32 devices in a mesh: dp: 8 (over z, y), frame: 4 (over x, core).
Axes of the slice: x: 2, y: 2, z: 4, core: 2. Of those that a mesh axis runs over, the one named last changes fastest.
Arguments:
- tokens: bfloat16 [16384, 768], P(('dp', 'frame')), may hold values from -6 to 6
- frames: bfloat16 [256, 1500, 768], P('dp', 'frame'), may hold values from -6 to 6
- cotangent: bfloat16 [16384, 768], P(('dp', 'frame')), may hold values from -6 to 6
- buckets: int32 [256], P('dp'), may hold values from 0 to 7, as said below
- lengths: int32 [256], P('dp'), may hold values from 0 to 448, as said below
- slot_of: int32 [96], replicated, may hold values from 0 to 127, as said below
- master: float32 [128, 128, 768], P('dp', None, 'frame'), may hold values from -3 to 3
- first_moment: float32 [128, 128, 768], P('dp', None, 'frame'), may hold values from -2 to 2
- second_moment: float32 [128, 128, 768], P('dp', None, 'frame'), may hold values from 0.01 to 0.1
- vectors: float32 [19, 768], replicated, may hold values from -3 to 3
- vector_first: float32 [19, 768], replicated, may hold values from -6 to 6
- vector_second: float32 [19, 768], replicated, may hold values from 0.05 to 0.5
Outputs:
- out_tokens: float32 [16384, 768], P(('dp', 'frame'))
- token_grads: float32 [16384, 768], P(('dp', 'frame'))
- matrix_grads: float32 [128, 128, 768], P('dp', None, 'frame')
- matrix_first: float32 [128, 128, 768], P('dp', None, 'frame')
- matrix_second: float32 [128, 128, 768], P('dp', None, 'frame')
- matrix_weights: float32 [128, 128, 768], P('dp', None, 'frame')
- vector_grads: float32 [19, 768], replicated
- vector_first_new: float32 [19, 768], replicated
- vector_second_new: float32 [19, 768], replicated
- vector_weights: float32 [19, 768], replicated
The draws below stay inside these ranges and needn't reach their ends.
Inputs may be any that keep to these rules, and one draw needn't show every extreme that they name: `buckets`: A device's slots take 8 units or fewer together, and some device takes exactly 8; the first slot of every device is taken; some slot has 7 units. `lengths`: 0 for an empty slot, else more than 64 (b - 1) and at most 64 b for the slot's bucket b; some slot has 448. `slot_of`: distinct slots; slot s belongs to dp index s // 16; some dp index owns 16 panels.
All inputs are finite; a program needn't handle non-finite values.
Results may differ from the reference program's by a relative error of at most 0.025.
The reference program's roundings to bfloat16 on the way count: a program that leaves them out, or rounds other values in their place, can miss the bound.
Values may be sent and summed in bfloat16 or wider, within the bound.
No kernel may reach another device: no remote copies, remote signals or barrier semaphores. Data moves between devices by JAX's collectives and lax.ppermute only.
A program may use at most 448 MiB of HBM per device.

```python
import math
import jax
import jax.numpy as jnp
from jax import lax

D = 768
HEADS = 12
FF = 3072
FRAMES = 1500
BLOCK = 64
PANEL = 128
STEP = 4
BLK_DEV = 8
HEAD = 64
TR_DEV = 8
TRANSCRIPTS = 256
TOKENS = 16384
PANELS = 96
CAP = 16
SLOTS = 128
VEC = 19


def slot_table(key):
    folded = jax.random.fold_in(key, 101)
    shuffled = jax.random.permutation(folded, SLOTS).astype(jnp.int32)
    position = jnp.zeros((SLOTS,), jnp.int32).at[shuffled].set(jnp.arange(SLOTS, dtype=jnp.int32))
    full_device = shuffled[0] // CAP
    sort_score = jnp.where(jnp.arange(SLOTS, dtype=jnp.int32) // CAP == full_device, 0, SLOTS) + position
    ordered = jnp.argsort(sort_score, stable=True).astype(jnp.int32)[:PANELS]
    mixing = jax.random.permutation(jax.random.fold_in(folded, 1), PANELS).astype(jnp.int32)
    return ordered[mixing]


def bucket_table(key):
    folded = jax.random.fold_in(key, 202)
    devices = TRANSCRIPTS // TR_DEV
    sizes_drawn = jax.random.randint(jax.random.fold_in(folded, 1), (devices, TR_DEV), 1, 3)
    full_device = jax.random.randint(jax.random.fold_in(folded, 2), (), 0, devices)
    filler = jnp.clip(BLK_DEV - 7 * jnp.arange(TR_DEV, dtype=jnp.int32), 0, 7)
    device_ids = jnp.arange(devices, dtype=jnp.int32)
    sizes_drawn = jnp.where(device_ids[:, None] == full_device, filler[None, :], sizes_drawn)
    running = jnp.cumsum(sizes_drawn, axis=1)
    bucket_units = jnp.where(running <= BLK_DEV, sizes_drawn, 0)
    extra_rows = jax.random.randint(jax.random.fold_in(folded, 3), (devices, TR_DEV), 1, BLOCK + 1)
    length_rows = jnp.where(bucket_units > 0, BLOCK * (bucket_units - 1) + extra_rows, 0)
    first_column = jnp.arange(TR_DEV, dtype=jnp.int32)[None, :] == 0
    length_rows = jnp.where((device_ids[:, None] == full_device) & first_column, 7 * BLOCK, length_rows)
    return (bucket_units.reshape(-1).astype(jnp.int32), length_rows.reshape(-1).astype(jnp.int32))


def panel_scales():
    per_matrix = D // PANEL
    square_count = 8 * per_matrix
    base_scale = D ** (-0.5)
    kind_scale = jnp.array([1.0, 1.5, 1.0, 4.2, 1.0, 2.0, 1.0, 4.2], jnp.float32) * base_scale
    panel_ids = jnp.arange(PANELS, dtype=jnp.int32)
    square_part = kind_scale[jnp.minimum(panel_ids // per_matrix, 7)]
    return jnp.where(panel_ids < square_count, square_part, jnp.where(panel_ids < square_count + FF // PANEL, base_scale, 1.6 * FF ** (-0.5)))


def draw_buckets(key, part):
    return bucket_table(key)[0]


def draw_lengths(key, part):
    return bucket_table(key)[1]


def draw_slot_of(key, part):
    return slot_table(key)


def draw_master(key, part):
    chosen = slot_table(key)
    key = jax.random.fold_in(key, 7)
    noise_draw = jax.random.truncated_normal(key, -4.0, 4.0, (SLOTS, PANEL, D), jnp.float32)
    slot_scale = jnp.full((SLOTS,), D ** (-0.5), jnp.float32).at[chosen].set(panel_scales())
    return noise_draw * slot_scale[:, None, None]


def draw_vectors(key, part):
    key = jax.random.fold_in(key, 303)
    row_total = 15 + FF // D
    row_ids = jnp.arange(row_total, dtype=jnp.int32)
    gain_rows = (row_ids == 0) | (row_ids == 5) | (row_ids == 10) | (row_ids == 13 + FF // D)
    spread_draw = jax.random.truncated_normal(key, -4.0, 4.0, (row_total, D), jnp.float32)
    return jnp.where(gain_rows[:, None], 1.0 + 0.25 * spread_draw, 0.3 * spread_draw)


def level_of(own_key, extent, split, least, largest):
    def one(dim, parts):
        draws = jax.random.uniform(jax.random.fold_in(jax.random.fold_in(own_key, 6), dim), (parts,), jnp.float32, least / len(split), largest / len(split))
        return jnp.repeat(jnp.exp(draws), extent[dim] // parts).reshape((-1,) + (1,) * (len(extent) - dim - 1))

    gain = one(*split[0])
    for cut in split[1:]:
        gain = gain * one(*cut)
    return gain


def noise(key, extent, width, reach, split=(), kind=jnp.bfloat16):
    drawn = width * jax.random.normal(key, extent, jnp.float32)
    if split:
        drawn = drawn * level_of(key, extent, split, -0.22, 0.18)
    return jnp.clip(drawn, -reach, reach).astype(kind)


def setup_inputs(seed: int = 0) -> dict:
    splits = jax.random.split(jax.random.key(seed), 13)
    return {
        "tokens": noise(splits[0], (TOKENS, D), 1.0, 6.0, ((0, 32),)),
        "frames": noise(splits[1], (TRANSCRIPTS, FRAMES, D), 1.0, 6.0, ((0, 8), (1, 4))),
        "cotangent": noise(splits[2], (TOKENS, D), 1.0, 6.0, ((0, 32),)),
        "buckets": draw_buckets(jax.random.fold_in(splits[12], 71), 0),
        "lengths": draw_lengths(jax.random.fold_in(splits[12], 71), 0),
        "slot_of": draw_slot_of(jax.random.fold_in(splits[12], 71), 0),
        "master": draw_master(jax.random.fold_in(splits[12], 71), 0),
        "first_moment": noise(splits[7], (SLOTS, PANEL, D), 0.15, 2.0, ((0, 8), (2, 4)), jnp.float32),
        "second_moment": jnp.clip(jnp.exp(math.log(0.1) - 2.3025851 * jax.random.uniform(splits[8], (SLOTS, PANEL, D), jnp.float32) ** level_of(splits[8], (SLOTS, PANEL, D), ((0, 8), (2, 4)), -0.2, 0.2)), 0.01, 0.1),
        "vectors": draw_vectors(jax.random.fold_in(splits[12], 71), 0),
        "vector_first": noise(splits[10], (VEC, D), 0.4, 6.0, (), jnp.float32),
        "vector_second": jnp.clip(jnp.exp(jax.random.uniform(splits[11], (VEC, D), jnp.float32, math.log(0.05), math.log(0.5))), 0.05, 0.5),
    }


EPS_NORM = 1e-05
EPS_ADAM = 1e-08
BETA_ONE = 0.5
BETA_TWO = 0.5
RATE_MATRIX = 0.04
RATE_VECTOR = 0.2
DECAY_MATRIX = 0.01
MASKED = -1e+30
HIGHEST_PRECISION = lax.Precision.HIGHEST

@jax.custom_vjp
def low(v):
    return lax.optimization_barrier(v.astype(jnp.bfloat16)).astype(jnp.float32)

@jax.custom_vjp
def low_back(v):
    return v

def low_keep(v):
    return (low(v), None)

def low_pass(kept, grad):
    return (grad,)

def back_keep(v):
    return (v, None)

def back_low(kept, grad):
    return (low(grad),)
low.defvjp(low_keep, low_pass)
low_back.defvjp(back_keep, back_low)

def round_both(values):
    return low_back(low(values))

def layer_norm(values, scaling, offset):
    average = lax.optimization_barrier(jnp.mean(values, axis=-1, keepdims=True))
    centred = values - average
    spread = lax.optimization_barrier(jnp.mean(centred * centred, axis=-1, keepdims=True))
    return centred * lax.rsqrt(spread + EPS_NORM) * scaling + offset

def matmul(operand, factor):
    return jnp.dot(operand, factor, precision=HIGHEST_PRECISION, preferred_element_type=jnp.float32)

def row_layout(bucket, length, row_count, block_rows):
    slot_count = bucket.shape[0]
    starts = (jnp.cumsum(bucket, dtype=jnp.int32) - bucket).astype(jnp.int32)
    row_ids = jnp.arange(row_count, dtype=jnp.int32)
    slot_ids = jnp.arange(slot_count, dtype=jnp.int32)
    block_ids = row_ids // block_rows
    inside = (block_ids[:, None] >= starts[None, :]) & (block_ids[:, None] < (starts + bucket)[None, :])
    member = jnp.where(jnp.any(inside, axis=1), lax.optimization_barrier(jnp.sum(jnp.where(inside, slot_ids[None, :], 0), axis=1, dtype=jnp.int32)), -1).astype(jnp.int32)
    live_rows = jnp.any(inside & (row_ids[:, None] - block_rows * starts[None, :] < length[None, :]), axis=1)
    block_owner = jnp.maximum(member.reshape(row_count // block_rows, block_rows)[:, 0], 0).astype(jnp.int32)
    return (member, live_rows, block_owner)

def adam_update(gradient, first_moment, second_moment, weight, step_rate, decay_rate):
    first_new = BETA_ONE * first_moment + (1.0 - BETA_ONE) * gradient
    second_new = BETA_TWO * second_moment + (1.0 - BETA_TWO) * gradient * gradient
    fix_one = 1.0 - BETA_ONE ** STEP
    fix_two = 1.0 - BETA_TWO ** STEP
    update = first_new / fix_one / (jnp.sqrt(second_new / fix_two) + EPS_ADAM)
    return (first_new, second_new, weight - step_rate * (update + decay_rate * weight))

def buffer_pass(params, packed):
    square, expand, contract, vectors = params
    inputs, frame_rows, bucket, length = packed
    encoded = frame_rows.astype(jnp.float32)
    row_count = inputs.shape[0]
    unit_count = row_count // BLOCK
    blocks_ff = FF // D
    query_scale = HEAD ** (-0.5)
    member, live_rows, block_owner = row_layout(bucket, length, row_count, BLOCK)
    row_ids = jnp.arange(row_count, dtype=jnp.int32)
    visible = (member[:, None] == member[None, :]) & (row_ids[None, :] <= row_ids[:, None]) & (live_rows[None, :] | (row_ids[None, :] == row_ids[:, None]))
    normed = low(layer_norm(inputs, vectors[0], vectors[1]))
    self_query = round_both(query_scale * (matmul(normed, square[0]) + vectors[2])).reshape(row_count, HEADS, HEAD)
    self_key = round_both(matmul(normed, square[1])).reshape(row_count, HEADS, HEAD)
    self_value = round_both(matmul(normed, square[2]) + vectors[3]).reshape(row_count, HEADS, HEAD)
    scores = low_back(jnp.einsum('qhd,khd->hqk', self_query, self_key, precision=HIGHEST_PRECISION))
    self_probs = low(jax.nn.softmax(jnp.where(visible[None], scores, MASKED), axis=-1))
    attended = round_both(jnp.einsum('hqk,khd->qhd', self_probs, self_value, precision=HIGHEST_PRECISION).reshape(row_count, D))
    first_sum = inputs + low_back(matmul(attended, square[3]) + vectors[4])
    crossed = low(layer_norm(first_sum, vectors[5], vectors[6]))
    cross_query = round_both(query_scale * (matmul(crossed, square[4]) + vectors[7]))
    cross_key = round_both(jnp.einsum('tfd,de->tfe', encoded, square[5], precision=HIGHEST_PRECISION))
    cross_value = round_both(jnp.einsum('tfd,de->tfe', encoded, square[6], precision=HIGHEST_PRECISION) + vectors[8])
    block_query = cross_query.reshape(unit_count, BLOCK, HEADS, HEAD)
    block_key = cross_key[block_owner].reshape(unit_count, FRAMES, HEADS, HEAD)
    block_value = cross_value[block_owner].reshape(unit_count, FRAMES, HEADS, HEAD)
    cross_scores = low_back(jnp.einsum('bqhd,bfhd->bhqf', block_query, block_key, precision=HIGHEST_PRECISION))
    cross_probs = low(jax.nn.softmax(cross_scores, axis=-1))
    cross_out = round_both(jnp.einsum('bhqf,bfhd->bqhd', cross_probs, block_value, precision=HIGHEST_PRECISION).reshape(row_count, D))
    second_sum = first_sum + low_back(matmul(cross_out, square[7]) + vectors[9])
    mlp_input = low(layer_norm(second_sum, vectors[10], vectors[11]))
    hidden_pre = low_back(jnp.einsum('rd,cde->rce', mlp_input, expand, precision=HIGHEST_PRECISION).reshape(row_count, FF) + vectors[12:12 + blocks_ff].reshape(FF))
    activated = low(jax.nn.gelu(hidden_pre, approximate=False))
    third_sum = second_sum + low_back(matmul(activated, contract) + vectors[12 + blocks_ff])
    result = layer_norm(third_sum, vectors[13 + blocks_ff], vectors[14 + blocks_ff])
    return result * live_rows[:, None].astype(jnp.float32)

def reference(tokens, frames, cotangent, buckets, lengths, slot_of, master, first_moment, second_moment, vectors, vector_first, vector_second):
    buffers = TRANSCRIPTS // TR_DEV
    row_count = tokens.shape[0] // buffers
    slot_ids = jnp.arange(SLOTS, dtype=jnp.int32)
    used_slots = jnp.any(slot_of[:, None] == slot_ids[None, :], axis=0)
    copies = lax.optimization_barrier(master.astype(jnp.bfloat16)).astype(jnp.float32)
    panels = copies[slot_of]
    square_count = 8 * D // PANEL
    expand_count = FF // PANEL
    square = panels[:square_count].reshape(8, D, D)
    expand = panels[square_count:square_count + expand_count].reshape(FF // D, D, D)
    contract = panels[square_count + expand_count:].reshape(FF, D)

    def forward(params, inputs):
        buffer_items = (inputs.reshape(buffers, row_count, D), frames.reshape(buffers, TR_DEV, FRAMES, D), buckets.reshape(buffers, TR_DEV), lengths.reshape(buffers, TR_DEV))
        per_buffer = jax.checkpoint(lambda packed: buffer_pass(params, packed))
        return lax.map(per_buffer, buffer_items).reshape(buffers * row_count, D)
    result, pullback = jax.vjp(forward, (square, expand, contract, vectors), tokens.astype(jnp.float32))
    gradients, token_grads = pullback(cotangent.astype(jnp.float32))
    grad_square, grad_expand, grad_contract, grad_vectors = gradients
    grad_scale = 1.0 / math.sqrt(TOKENS)
    grad_panels = jnp.concatenate([grad_square.reshape(-1, PANEL, D), grad_expand.reshape(-1, PANEL, D), grad_contract.reshape(-1, PANEL, D)], axis=0) * grad_scale
    matrix_grads = jnp.zeros((SLOTS, PANEL, D), jnp.float32).at[slot_of].set(grad_panels)
    matrix_first, matrix_second, matrix_weights = adam_update(matrix_grads, first_moment, second_moment, master, RATE_MATRIX, DECAY_MATRIX)
    slot_mask = used_slots[:, None, None]
    matrix_first = jnp.where(slot_mask, matrix_first, 0.0)
    matrix_second = jnp.where(slot_mask, matrix_second, 0.0)
    matrix_weights = jnp.where(slot_mask, matrix_weights, 0.0)
    vector_grads = grad_vectors * grad_scale
    vector_first_new, vector_second_new, vector_weights = adam_update(vector_grads, vector_first, vector_second, vectors, RATE_VECTOR, 0.0)
    return (result, token_grads, matrix_grads, matrix_first, matrix_second, matrix_weights, vector_grads, vector_first_new, vector_second_new, vector_weights)
```

```python
import functools
import math

import jax
import jax.numpy as jnp
from jax import lax
from jax.experimental import pallas as pl
from jax.experimental.pallas import tpu as pltpu
from jax.sharding import PartitionSpec as P

D = 768
HEADS = 12
HEAD = 64
FF = 3072
BLOCK = 64
PANEL = 128
STEP = 4
WIDE = 256
GROUPS = D // WIDE
ROWS = 6
MATS = 16
PARTIAL = 544
PACKED = 560

EPS_NORM = 1e-05
EPS_ADAM = 1e-08
BETA_ONE = 0.5
BETA_TWO = 0.5
RATE_MATRIX = 0.04
RATE_VECTOR = 0.2
DECAY_MATRIX = 0.01
MASKED = -1e30
SCALE = HEAD**-0.5

BF = jnp.bfloat16
F32 = jnp.float32
VMEM_LIMIT = 60 * 1024 * 1024


def dot_nt(a, b):
    return lax.dot_general(a, b, (((1,), (1,)), ((), ())), preferred_element_type=F32)


def dot_nn(a, b):
    return lax.dot_general(a, b, (((1,), (0,)), ((), ())), preferred_element_type=F32)


def eye():
    return (
        lax.broadcasted_iota(jnp.int32, (WIDE, WIDE), 0)
        == lax.broadcasted_iota(jnp.int32, (WIDE, WIDE), 1)
    ).astype(BF)


def turned(x, unit):
    parts = [
        dot_nt(unit, x[:, s : s + WIDE]).astype(BF) for s in range(0, x.shape[1], WIDE)
    ]
    return parts[0] if len(parts) == 1 else jnp.concatenate(parts, axis=0)


def head_mask():
    return (
        lax.broadcasted_iota(jnp.int32, (WIDE, WIDE), 0) >> 6
        == lax.broadcasted_iota(jnp.int32, (WIDE, WIDE), 1) >> 6
    )


def row_pick():
    return (
        lax.broadcasted_iota(jnp.int32, (HEAD, WIDE), 0)
        == lax.broadcasted_iota(jnp.int32, (HEAD, WIDE), 1) & (HEAD - 1)
    ).astype(BF)


def thirds(x):
    high = x.astype(BF)
    rest = x - high.astype(F32)
    middle = rest.astype(BF)
    return high, middle, (rest - middle.astype(F32)).astype(BF)


def norm_parts(v):
    average = jnp.mean(v, axis=-1, keepdims=True)
    centred = v - average
    inverse = lax.rsqrt(jnp.mean(centred * centred, axis=-1, keepdims=True) + EPS_NORM)
    return centred * inverse, inverse


def norm_back(e, unit_rows, inverse, gain):
    f = e * gain
    lean = jnp.mean(f, axis=-1, keepdims=True)
    slant = jnp.mean(f * unit_rows, axis=-1, keepdims=True)
    return (f - lean - unit_rows * slant) * inverse


def column_sum(x):
    return jnp.sum(x, axis=0, keepdims=True)


def matrix_copies(tiles, where, matrix, target, sem):
    copies = []
    for r in range(ROWS):
        for f in range(4):
            copies.append(
                pltpu.make_async_copy(
                    tiles.at[where[(matrix * ROWS + r) * 4 + f]],
                    target.at[pl.ds(f * 192, 192), pl.ds(r * PANEL, PANEL)],
                    sem,
                )
            )
    return copies


def gradient_copies(staged, keep, send, slot, me, sem):
    copies = []
    for relative in range(4):
        f = relative ^ me
        target = send if relative & 1 else keep
        for r in range(ROWS):
            copies.append(
                pltpu.make_async_copy(
                    staged.at[pl.ds(pl.multiple_of(f * 192, 64), 192), pl.ds(r * PANEL, PANEL)],
                    target.at[relative >> 1, slot * ROWS + r],
                    sem,
                )
            )
    return copies


def start_all(copies):
    for copy in copies:
        copy.start()


def wait_all(copies):
    for copy in copies:
        copy.wait()


def front_kernel(
    where, tokens, vectors, member_column, live_column, member_row, tiles,
    sum_one, cross_query, query, key, value, attended, lse,
    weights, bias, sems,
):
    loads = [
        matrix_copies(tiles, where, i, weights.at[i], sems.at[i]) for i in range(5)
    ]
    for load in loads:
        start_all(load)
    unit = eye()
    count = tokens.shape[0]
    key_ids = lax.broadcasted_iota(jnp.int32, (count, count), 0)
    row_ids = lax.broadcasted_iota(jnp.int32, (count, count), 1)
    seen = (
        (member_column[...] == member_row[...])
        & (key_ids <= row_ids)
        & ((live_column[...] > 0) | (key_ids == row_ids))
    )
    bias[...] = jnp.where(seen, 0.0, MASKED)
    x = tokens[...].astype(F32)
    a = (norm_parts(x)[0] * vectors[0:1] + vectors[1:2]).astype(BF)
    wait_all(loads[0])
    query[...] = (SCALE * (dot_nt(a, weights[0]) + vectors[2:3])).astype(BF)
    wait_all(loads[1])
    key[...] = dot_nt(a, weights[1]).astype(BF)
    wait_all(loads[2])
    value[...] = (dot_nt(a, weights[2]) + vectors[3:4]).astype(BF)
    lanes = lax.broadcasted_iota(jnp.int32, (1, WIDE), 1) >> 6
    lse[...] = jnp.zeros_like(lse)
    for g in range(GROUPS):
        cols = pl.ds(g * WIDE, WIDE)
        q, k = query[:, cols], key[:, cols]
        v_turned = turned(value[:, cols], unit)
        outs = []
        for h in range(4):
            masked_q = jnp.where(lanes == h, q, jnp.zeros_like(q))
            scores = dot_nt(k, masked_q) + bias[...]
            top = jnp.max(scores, axis=0, keepdims=True)
            p = jnp.exp(scores - top)
            total = jnp.sum(p, axis=0, keepdims=True)
            out = dot_nn(v_turned[h * HEAD : (h + 1) * HEAD], p.astype(BF))
            outs.append((out * (1.0 / total)).astype(BF))
            lse[g * 4 + h : g * 4 + h + 1] = top + jnp.log(total)
        attended[:, cols] = turned(jnp.concatenate(outs, axis=0), unit)
    wait_all(loads[3])
    h1 = x + (dot_nt(attended[...], weights[3]) + vectors[4:5])
    sum_one[...] = h1
    c = (norm_parts(h1)[0] * vectors[5:6] + vectors[6:7]).astype(BF)
    wait_all(loads[4])
    cross_query[...] = (SCALE * (dot_nt(c, weights[4]) + vectors[7:8])).astype(BF)


def tables_kernel(act, where, frames, vectors, tiles, key_table, value_table, weights, sems):
    step = pl.program_id(0)

    @pl.when(step == 0)
    def _():
        loads = [
            matrix_copies(tiles, where, 5 + i, weights.at[i], sems.at[i]) for i in range(2)
        ]
        for load in loads:
            start_all(load)
        for load in loads:
            wait_all(load)

    @pl.when(step < act[0])
    def _():
        f = frames[0]
        key_table[0] = dot_nt(f, weights[0]).astype(BF)
        value_table[0] = (dot_nt(f, weights[1]) + vectors[8:9]).astype(BF)


def pad_rows(scores, fill):
    half = scores.shape[0] // 2
    odd = lax.broadcasted_iota(jnp.int32, (16, 1), 0) + (half - 16) >= 375
    parts = []
    for s in (0, half):
        parts.append(scores[s : s + half - 16])
        parts.append(jnp.where(odd, fill, scores[s + half - 16 : s + half]))
    return jnp.concatenate(parts, axis=0)


def each_unit(info, body):
    step = pl.program_id(0)
    first, mine = info[10 + step], info[18 + step]
    rest = jnp.where(step == 0, 8 - info[1], 0)

    def one(j, state):
        body(jnp.where(j < mine, first + j, info[1] + j - mine))
        return state

    lax.fori_loop(0, mine + rest, one, 0)


def spread_heads(x, mask):
    return jnp.where(mask, jnp.concatenate([x] * 4, axis=0), jnp.zeros((), x.dtype))


def cross_forward_kernel(info, query, key_table, value_table, out, value_turned, lse):
    step = pl.program_id(0)

    @pl.when(step < info[0])
    def _():
        unit, mask, pick = eye(), head_mask(), row_pick()
        for g in range(GROUPS):
            cols = pl.ds(g * WIDE, WIDE)
            value_turned[g] = turned(value_table[0, :, cols], unit)

        def body(u):
            rows = pl.ds(pl.multiple_of(u * BLOCK, BLOCK), BLOCK)
            for g in range(GROUPS):
                cols = pl.ds(g * WIDE, WIDE)
                wide_q = spread_heads(query[rows, cols], mask)
                scores = pad_rows(dot_nt(key_table[0, :, cols], wide_q), MASKED)
                top = jnp.max(scores, axis=0, keepdims=True)
                p = jnp.exp(scores - top)
                total = jnp.sum(p, axis=0, keepdims=True)
                o = dot_nn(value_turned[g], p.astype(BF)) * (1.0 / total)
                o = jnp.where(mask, o, 0.0).astype(BF)
                out[rows, cols] = dot_nt(pick, o).astype(BF)
                lse[pl.ds(u, 1), cols] = top + jnp.log(total)

        each_unit(info, body)

    @pl.when(step == pl.num_programs(0) - 1)
    def _():
        parts = [t.astype(F32) for t in thirds(lse[...])]
        parts.append(jnp.zeros_like(parts[0]))
        out[512:PARTIAL] = jnp.concatenate(parts, axis=0).astype(BF)


def cross_backward_kernel(
    info, query, packed, key_table, value_table, frames, grad_key_in, grad_value_in, bias_in,
    grad_query, grad_key, grad_value, bias_grad,
    key_turned, key_sum, value_sum, lse, delta,
):
    step = pl.program_id(0)

    @pl.when(step == 0)
    def _():
        grad_key[...] = grad_key_in[...]
        grad_value[...] = grad_value_in[...]
        bias_grad[...] = bias_in[...]
        extra = packed[512:PACKED].astype(F32)
        lse[...] = extra[0:8] + extra[8:16] + extra[16:24]
        delta[...] = extra[24:32] + extra[32:40] + extra[40:48]

    @pl.when(step < info[0])
    def _():
        unit, mask, pick = eye(), head_mask(), row_pick()
        for g in range(GROUPS):
            cols = pl.ds(g * WIDE, WIDE)
            key_turned[g] = turned(key_table[0, :, cols], unit)
        key_sum[...] = jnp.zeros_like(key_sum)
        value_sum[...] = jnp.zeros_like(value_sum)

        def body(u):
            rows = pl.ds(pl.multiple_of(u * BLOCK, BLOCK), BLOCK)
            for g in range(GROUPS):
                cols = pl.ds(g * WIDE, WIDE)
                wide_q = spread_heads(query[rows, cols], mask)
                wide_o = spread_heads(packed[rows, cols], mask)
                scores = dot_nt(key_table[0, :, cols], wide_q)
                p = pad_rows(jnp.exp(scores - lse[pl.ds(u, 1), cols]), 0.0)
                dp = dot_nt(value_table[0, :, cols], wide_o)
                ds = (p * (dp - delta[pl.ds(u, 1), cols])).astype(BF)
                value_sum[:, cols] += dot_nn(p.astype(BF), wide_o)
                key_sum[:, cols] += dot_nn(ds, wide_q)
                dq = jnp.where(mask, dot_nn(key_turned[g], ds), 0.0).astype(BF)
                grad_query[rows, cols] = dot_nt(pick, dq).astype(BF)

        each_unit(info, body)
        f = frames[0]
        for g in range(GROUPS):
            cols = pl.ds(g * WIDE, WIDE)
            grad_key[cols, :] += dot_nn(turned(key_sum[:, cols].astype(BF), unit), f)
            low = value_sum[:, cols].astype(BF)
            grad_value[cols, :] += dot_nn(turned(low, unit), f)
            bias_grad[0:1, cols] += column_sum(low.astype(F32))


def middle_kernel(
    where, me, sum_one, own, other, vectors, live, cotangent, tiles,
    out_tokens, grad_two, packed, vector_grads, keep, send,
    weights, hidden, act, staged, third, merged, sems, out_sem,
):
    count = sum_one.shape[0]
    loads = {
        m: matrix_copies(tiles, where, m, weights.at[m - 7], sems.at[m - 7]) for m in range(7, 16)
    }
    for load in loads.values():
        start_all(load)
    unit, mask, pick = eye(), head_mask(), row_pick()
    lse_own = own[512:536].astype(F32)
    lse_other = other[512:536].astype(F32)
    lse_own = lse_own[0:8] + lse_own[8:16] + lse_own[16:24]
    lse_other = lse_other[0:8] + lse_other[8:16] + lse_other[16:24]
    top = jnp.maximum(lse_own, lse_other)
    weight_own = jnp.exp(lse_own - top)
    weight_other = jnp.exp(lse_other - top)
    total = weight_own + weight_other
    share = weight_own / total
    lse = top + jnp.log(total)
    for u in range(count // BLOCK):
        rows = pl.ds(u * BLOCK, BLOCK)
        for g in range(GROUPS):
            cols = pl.ds(g * WIDE, WIDE)
            part = share[u : u + 1, g * WIDE : (g + 1) * WIDE]
            high = part.astype(BF)
            low = (part - high.astype(F32)).astype(BF)
            none = jnp.zeros((), BF)
            factor = dot_nt(pick, jnp.where(mask, high, none)) + dot_nt(
                pick, jnp.where(mask, low, none)
            )
            first, second = own[rows, cols].astype(F32), other[rows, cols].astype(F32)
            merged[rows, cols] = second + factor * (first - second)
    cross_out = merged[...].astype(BF)
    wait_all(loads[7])
    h2 = sum_one[...] + (dot_nt(cross_out, weights[0]) + vectors[9:10])
    unit_three, inverse_three = norm_parts(h2)
    m = (unit_three * vectors[10:11] + vectors[11:12]).astype(BF)
    third[...] = h2 + vectors[16:17]
    for c in range(4):
        wait_all(loads[8 + c])
        wait_all(loads[12 + c])

    def ahead(c, state):
        u = dot_nt(m, weights[1 + c]) + vectors[pl.ds(12 + c, 1)]
        hidden[c] = u
        g = (u * (0.5 * (1.0 + lax.erf(u * math.sqrt(0.5))))).astype(BF)
        act[c] = g
        third[...] += dot_nt(g, weights[5 + c])
        return state

    lax.fori_loop(0, 4, ahead, 0)
    unit_last, inverse_last = norm_parts(third[...])
    alive = live[...]
    out_tokens[...] = (unit_last * vectors[17:18] + vectors[18:19]) * alive
    e = cotangent[...].astype(F32) * alive
    vector_grads[...] = jnp.zeros_like(vector_grads)
    vector_grads[8:9] = column_sum(e * unit_last)
    vector_grads[9:10] = column_sum(e)
    dh3 = norm_back(e, unit_last, inverse_last, vectors[17:18])
    third[...] = dh3
    e3 = dh3.astype(BF)
    vector_grads[7:8] = column_sum(e3.astype(F32))
    e3_turned = turned(e3, unit)
    grad_two[...] = jnp.zeros_like(grad_two)

    def back(c, state):
        staged[5 + c] = dot_nn(e3_turned, act[c]).astype(BF)
        start_all(gradient_copies(staged.at[5 + c], keep, send, 5 + c, me[0], out_sem))
        u = hidden[c]
        slope = 0.5 * (1.0 + lax.erf(u * math.sqrt(0.5))) + u * (
            jnp.exp(-0.5 * u * u) * (1.0 / math.sqrt(2.0 * math.pi))
        )
        du = (dot_nn(e3, weights[5 + c]) * slope).astype(BF)
        vector_grads[pl.ds(3 + c, 1)] = column_sum(du.astype(F32))
        staged[1 + c] = dot_nn(turned(du, unit), m).astype(BF)
        start_all(gradient_copies(staged.at[1 + c], keep, send, 1 + c, me[0], out_sem))
        grad_two[...] += dot_nn(du, weights[1 + c])
        return state

    lax.fori_loop(0, 4, back, 0)
    dm = grad_two[...]
    vector_grads[1:2] = column_sum(dm * unit_three)
    vector_grads[2:3] = column_sum(dm)
    dh2 = third[...] + norm_back(dm, unit_three, inverse_three, vectors[10:11])
    grad_two[...] = dh2
    e2 = dh2.astype(BF)
    vector_grads[0:1] = column_sum(e2.astype(F32))
    staged[0] = dot_nn(turned(e2, unit), cross_out).astype(BF)
    start_all(gradient_copies(staged.at[0], keep, send, 0, me[0], out_sem))
    packed[0:512] = dot_nn(e2, weights[0]).astype(BF)
    ones = jnp.ones((8, WIDE), BF)
    deltas = []
    for u in range(count // BLOCK):
        rows = pl.ds(u * BLOCK, BLOCK)
        line = []
        for g in range(GROUPS):
            cols = pl.ds(g * WIDE, WIDE)
            product = packed[rows, cols].astype(F32) * merged[rows, cols]
            high, middle, low = (spread_heads(t, mask) for t in thirds(product))
            line.append((dot_nt(ones, high) + dot_nt(ones, middle) + dot_nt(ones, low))[0:1])
        deltas.append(jnp.concatenate(line, axis=1))
    delta = jnp.concatenate(deltas, axis=0)
    extra = [t.astype(F32) for t in thirds(lse)] + [t.astype(F32) for t in thirds(delta)]
    packed[512:PACKED] = jnp.concatenate(extra, axis=0).astype(BF)
    for i in range(9):
        wait_all(gradient_copies(staged.at[i], keep, send, i, me[0], out_sem))


def last_kernel(
    where, me, tokens, sum_one, grad_two, query, key, value, attended, lse, own, other, vectors,
    member_column, live_column, member_row, tiles,
    token_grads, vector_grads, keep, send,
    weights, staged, bias, grad_att, grad_q, grad_q_turned, grad_k, grad_v, sems, out_sem,
):
    order = (4, 3, 0, 1, 2)
    loads = [
        matrix_copies(tiles, where, m, weights.at[i], sems.at[i]) for i, m in enumerate(order)
    ]
    for load in loads:
        start_all(load)
    unit = eye()
    count = tokens.shape[0]
    key_ids = lax.broadcasted_iota(jnp.int32, (count, count), 0)
    row_ids = lax.broadcasted_iota(jnp.int32, (count, count), 1)
    seen = (
        (member_column[...] == member_row[...])
        & (key_ids <= row_ids)
        & ((live_column[...] > 0) | (key_ids == row_ids))
    )
    bias[...] = jnp.where(seen, 0.0, MASKED)

    def put(slot, value_):
        staged[slot] = value_.astype(BF)
        start_all(gradient_copies(staged.at[slot], keep, send, slot, me[0], out_sem))

    ecq = (own[...].astype(F32) + other[...].astype(F32)).astype(BF) * jnp.asarray(SCALE, BF)
    vector_grads[...] = jnp.zeros_like(vector_grads)
    vector_grads[7:8] = column_sum(ecq.astype(F32))
    unit_two, inverse_two = norm_parts(sum_one[...])
    c = (unit_two * vectors[5:6] + vectors[6:7]).astype(BF)
    put(0, dot_nn(turned(ecq, unit), c))
    wait_all(loads[0])
    dc = dot_nn(ecq, weights[0])
    vector_grads[5:6] = column_sum(dc * unit_two)
    vector_grads[6:7] = column_sum(dc)
    dh1 = grad_two[...] + norm_back(dc, unit_two, inverse_two, vectors[5:6])
    token_grads[...] = dh1
    e1 = dh1.astype(BF)
    vector_grads[4:5] = column_sum(e1.astype(F32))
    put(1, dot_nn(turned(e1, unit), attended[...]))
    wait_all(loads[1])
    grad_att[...] = dot_nn(e1, weights[1]).astype(BF)
    lanes = lax.broadcasted_iota(jnp.int32, (1, WIDE), 1) >> 6
    for g in range(GROUPS):
        cols = pl.ds(g * WIDE, WIDE)
        q, k, v, do = query[:, cols], key[:, cols], value[:, cols], grad_att[:, cols]
        k_turned = turned(k, unit)
        dk = jnp.zeros((count, WIDE), F32)
        dv = jnp.zeros((count, WIDE), F32)
        for h in range(4):
            none = jnp.zeros_like(q)
            masked_q = jnp.where(lanes == h, q, none)
            masked_o = jnp.where(lanes == h, do, none)
            scores = dot_nt(k, masked_q) + bias[...]
            p = jnp.exp(scores - lse[g * 4 + h : g * 4 + h + 1])
            dp = dot_nt(v, masked_o)
            drift = jnp.sum(p * dp, axis=0, keepdims=True)
            ds = (p * (dp - drift)).astype(BF)
            dv = dv + dot_nn(p.astype(BF), masked_o)
            dk = dk + dot_nn(ds, masked_q)
            dq = dot_nn(k_turned[h * HEAD : (h + 1) * HEAD], ds).astype(BF)
            spot = g * WIDE + h * HEAD
            grad_q_turned[spot : spot + HEAD] = dq * jnp.asarray(SCALE, BF)
        grad_k[:, cols] = dk.astype(BF)
        grad_v[:, cols] = dv.astype(BF)
        grad_q[:, cols] = turned(grad_q_turned[cols, :], unit)
    x = tokens[...].astype(F32)
    unit_one, inverse_one = norm_parts(x)
    a = (unit_one * vectors[0:1] + vectors[1:2]).astype(BF)
    vector_grads[2:3] = column_sum(grad_q[...].astype(F32))
    vector_grads[3:4] = column_sum(grad_v[...].astype(F32))
    put(2, dot_nn(grad_q_turned[...], a))
    put(3, dot_nn(turned(grad_k[...], unit), a))
    put(4, dot_nn(turned(grad_v[...], unit), a))
    wait_all(loads[2])
    wait_all(loads[3])
    wait_all(loads[4])
    da = (
        dot_nn(grad_q[...], weights[2])
        + dot_nn(grad_k[...], weights[3])
        + dot_nn(grad_v[...], weights[4])
    )
    vector_grads[0:1] = column_sum(da * unit_one)
    vector_grads[1:2] = column_sum(da)
    token_grads[...] += norm_back(da, unit_one, inverse_one, vectors[0:1])
    for i in range(5):
        wait_all(gradient_copies(staged.at[i], keep, send, i, me[0], out_sem))


SMEM = pl.BlockSpec(memory_space=pltpu.SMEM)
WHOLE = pl.BlockSpec(memory_space=pltpu.VMEM)
AWAY = pl.BlockSpec(memory_space=pl.ANY)
PARAMS = pltpu.CompilerParams(vmem_limit_bytes=VMEM_LIMIT)


def shape(*dims, dtype=BF):
    return jax.ShapeDtypeStruct(dims, dtype)


def call_front(where, tokens, vectors, layout, tiles):
    count = tokens.shape[0]
    return pl.pallas_call(
        front_kernel,
        out_shape=(
            shape(count, D, dtype=F32),
            *(shape(count, D) for _ in range(5)),
            shape(16, count, dtype=F32),
        ),
        in_specs=[SMEM, WHOLE, WHOLE, WHOLE, WHOLE, WHOLE, AWAY],
        out_specs=(WHOLE,) * 7,
        scratch_shapes=[
            pltpu.VMEM((5, D, D), BF),
            pltpu.VMEM((count, count), F32),
            pltpu.SemaphoreType.DMA((5,)),
        ],
        compiler_params=PARAMS,
        name="front",
    )(where, tokens, vectors, *layout, tiles)


def call_tables(act, where, frames, vectors, tiles):
    slots, extent, _ = frames.shape

    def place(i, act, where):
        return (act[1 + i], 0, 0)

    block = pl.BlockSpec((1, extent, D), place)
    return pl.pallas_call(
        tables_kernel,
        out_shape=(shape(slots, extent, D),) * 2,
        grid_spec=pltpu.PrefetchScalarGridSpec(
            num_scalar_prefetch=2,
            grid=(slots,),
            in_specs=[block, WHOLE, AWAY],
            out_specs=(block, block),
            scratch_shapes=[pltpu.VMEM((2, D, D), BF), pltpu.SemaphoreType.DMA((2,))],
        ),
        compiler_params=PARAMS,
        name="tables",
    )(act, where, frames, vectors, tiles)


def whole_spec(*dims):
    return pl.BlockSpec(dims, lambda i, info: (0,) * len(dims))


def call_cross_forward(info, query, key_table, value_table, base):
    count, extent = query.shape[0], key_table.shape[1]
    slots = 8
    block = pl.BlockSpec((1, extent, D), lambda i, info: (base + info[2 + i], 0, 0))
    return pl.pallas_call(
        cross_forward_kernel,
        out_shape=shape(PARTIAL, D),
        grid_spec=pltpu.PrefetchScalarGridSpec(
            num_scalar_prefetch=1,
            grid=(slots,),
            in_specs=[whole_spec(count, D), block, block],
            out_specs=whole_spec(PARTIAL, D),
            scratch_shapes=[
                pltpu.VMEM((GROUPS, WIDE, extent), BF),
                pltpu.VMEM((8, D), F32),
            ],
        ),
        compiler_params=PARAMS,
        name="cross_forward",
    )(info, query, key_table, value_table)


def call_cross_backward(info, query, packed, key_table, value_table, frames, sums, base):
    count, extent = query.shape[0], key_table.shape[1]
    slots = 8
    block = pl.BlockSpec((1, extent, D), lambda i, info: (base + info[2 + i], 0, 0))
    return pl.pallas_call(
        cross_backward_kernel,
        out_shape=(
            shape(count, D),
            shape(D, D, dtype=F32),
            shape(D, D, dtype=F32),
            shape(8, D, dtype=F32),
        ),
        grid_spec=pltpu.PrefetchScalarGridSpec(
            num_scalar_prefetch=1,
            grid=(slots,),
            in_specs=[
                whole_spec(count, D),
                whole_spec(PACKED, D),
                block,
                block,
                block,
                whole_spec(D, D),
                whole_spec(D, D),
                whole_spec(8, D),
            ],
            out_specs=(
                whole_spec(count, D),
                whole_spec(D, D),
                whole_spec(D, D),
                whole_spec(8, D),
            ),
            scratch_shapes=[
                pltpu.VMEM((GROUPS, WIDE, extent), BF),
                pltpu.VMEM((extent, D), F32),
                pltpu.VMEM((extent, D), F32),
                pltpu.VMEM((8, D), F32),
                pltpu.VMEM((8, D), F32),
            ],
        ),
        compiler_params=PARAMS,
        name="cross_backward",
    )(info, query, packed, key_table, value_table, frames, *sums)


def call_middle(where, me, sum_one, own, other, vectors, live, cotangent, tiles):
    count = sum_one.shape[0]
    part = shape(2, 9 * ROWS, 192, PANEL)
    return pl.pallas_call(
        middle_kernel,
        out_shape=(
            shape(count, D, dtype=F32),
            shape(count, D, dtype=F32),
            shape(PACKED, D),
            shape(16, D, dtype=F32),
            part,
            part,
        ),
        in_specs=[SMEM, SMEM, WHOLE, WHOLE, WHOLE, WHOLE, WHOLE, WHOLE, AWAY],
        out_specs=(WHOLE, WHOLE, WHOLE, WHOLE, AWAY, AWAY),
        scratch_shapes=[
            pltpu.VMEM((9, D, D), BF),
            pltpu.VMEM((4, count, D), F32),
            pltpu.VMEM((4, count, D), BF),
            pltpu.VMEM((9, D, D), BF),
            pltpu.VMEM((count, D), F32),
            pltpu.VMEM((count, D), F32),
            pltpu.SemaphoreType.DMA((9,)),
            pltpu.SemaphoreType.DMA,
        ],
        compiler_params=PARAMS,
        name="middle",
    )(where, me, sum_one, own, other, vectors, live, cotangent, tiles)


def call_last(where, me, tokens, sum_one, grad_two, saved, own, other, vectors, layout, tiles):
    count = tokens.shape[0]
    part = shape(2, 5 * ROWS, 192, PANEL)
    return pl.pallas_call(
        last_kernel,
        out_shape=(shape(count, D, dtype=F32), shape(8, D, dtype=F32), part, part),
        in_specs=[SMEM, SMEM] + [WHOLE] * 14 + [AWAY],
        out_specs=(WHOLE, WHOLE, AWAY, AWAY),
        scratch_shapes=[
            pltpu.VMEM((5, D, D), BF),
            pltpu.VMEM((5, D, D), BF),
            pltpu.VMEM((count, count), F32),
            pltpu.VMEM((count, D), BF),
            pltpu.VMEM((count, D), BF),
            pltpu.VMEM((D, count), BF),
            pltpu.VMEM((count, D), BF),
            pltpu.VMEM((count, D), BF),
            pltpu.SemaphoreType.DMA((5,)),
            pltpu.SemaphoreType.DMA,
        ],
        compiler_params=PARAMS,
        name="last",
    )(where, me, tokens, sum_one, grad_two, *saved, own, other, vectors, *layout, tiles)


def row_layout(bucket, length, row_count):
    starts = jnp.cumsum(bucket, dtype=jnp.int32) - bucket
    row_ids = jnp.arange(row_count, dtype=jnp.int32)
    slot_ids = jnp.arange(bucket.shape[0], dtype=jnp.int32)
    block_ids = row_ids // BLOCK
    inside = (block_ids[:, None] >= starts[None, :]) & (
        block_ids[:, None] < (starts + bucket)[None, :]
    )
    member = jnp.where(
        jnp.any(inside, axis=1),
        jnp.sum(jnp.where(inside, slot_ids[None, :], 0), axis=1, dtype=jnp.int32),
        -1,
    )
    live = jnp.any(
        inside & (row_ids[:, None] - BLOCK * starts[None, :] < length[None, :]), axis=1
    )
    return member, live


def packed_slots(bucket):
    count = bucket.shape[0]
    ids = jnp.arange(count, dtype=jnp.int32)
    taken = bucket > 0
    number = jnp.sum(taken, dtype=jnp.int32)
    rank = jnp.cumsum(taken, dtype=jnp.int32) - 1
    step = jnp.minimum(ids, number - 1)
    hit = (rank[None, :] == step[:, None]) & taken[None, :]

    def pick(values):
        return jnp.sum(jnp.where(hit, values[None, :], 0), axis=1, dtype=jnp.int32)

    starts = jnp.cumsum(bucket, dtype=jnp.int32) - bucket
    return number, pick(ids), pick(starts), pick(bucket)


def adam_update(gradient, first_moment, second_moment, weight, step_rate, decay_rate):
    first_new = BETA_ONE * first_moment + (1.0 - BETA_ONE) * gradient
    second_new = BETA_TWO * second_moment + (1.0 - BETA_TWO) * gradient * gradient
    fix_one = 1.0 - BETA_ONE**STEP
    fix_two = 1.0 - BETA_TWO**STEP
    update = first_new / fix_one / (jnp.sqrt(second_new / fix_two) + EPS_ADAM)
    return (first_new, second_new, weight - step_rate * (update + decay_rate * weight))


def swap(x, bit):
    return lax.ppermute(x, "frame", [(i, i ^ bit) for i in range(4)])


def reduced(keep, send):
    mine = (keep.astype(F32) + swap(send, 1).astype(F32)).astype(BF)
    quarter = (mine[0].astype(F32) + swap(mine[1], 2).astype(F32)).astype(BF)
    return lax.psum(quarter, "dp")


def body(
    tokens, frames, cotangent, buckets, lengths, slot_of, master, first_moment, second_moment,
    vectors, vector_first, vector_second,
):
    row_count = tokens.shape[0]
    group_count = lax.axis_size("dp")
    frame_count = lax.axis_size("frame")
    me = lax.axis_index("frame")
    group_index = lax.axis_index("dp")
    cap = master.shape[0]
    panel_total = slot_of.shape[0]
    slots = buckets.shape[0] // frame_count
    extent = frames.shape[1]

    tiles = lax.all_gather(
        master.astype(BF).transpose(0, 2, 1)[None], ("dp", "frame"), axis=0, tiled=True
    )
    tiles = tiles.reshape(group_count * frame_count * cap, master.shape[2], PANEL)
    quarter_ids = jnp.arange(frame_count, dtype=jnp.int32)
    where = (
        ((slot_of // cap)[:, None] * frame_count + quarter_ids[None, :]) * cap
        + (slot_of % cap)[:, None]
    ).reshape(-1)

    core, far = me & 1, me >> 1
    room = (extent + 15) // 16 * 16
    by_buffer = frames.reshape(2, 2, slots, extent, D)

    def halves(bit):
        part = lax.dynamic_index_in_dim(by_buffer, bit, 1, False)
        first = lax.dynamic_index_in_dim(part, far, 0, False)
        second = lax.dynamic_index_in_dim(part, 1 - far, 0, False)
        return jnp.pad(
            jnp.concatenate([first, second], axis=0), ((0, 0), (0, room - extent), (0, 0))
        )

    all_frames = jnp.concatenate([halves(core), swap(halves(1 - core), 1)], axis=1)

    by_device = buckets.reshape(frame_count, slots)
    own_bucket = lax.dynamic_index_in_dim(by_device, me, 0, False)
    far_bucket = lax.dynamic_index_in_dim(by_device, me ^ 2, 0, False)
    own_length = lax.dynamic_index_in_dim(lengths.reshape(frame_count, slots), me, 0, False)
    infos = []
    for bucket in (own_bucket, far_bucket):
        number, places, starts, units = packed_slots(bucket)
        infos.append(
            jnp.concatenate([jnp.stack([number, jnp.sum(bucket)]), places, starts, units])
        )
    both = packed_slots(jnp.concatenate([own_bucket, far_bucket]))
    act = jnp.concatenate([both[0][None], both[1]])
    member, live = row_layout(own_bucket, own_length, row_count)
    layout = (member[:, None], live.astype(jnp.int32)[:, None], member[None, :])

    key_table, value_table = call_tables(act, where, all_frames, vectors, tiles)
    sum_one, cross_query, *saved = call_front(where, tokens, vectors, layout, tiles)
    far_query = swap(cross_query, 2)
    own_part = call_cross_forward(infos[0], cross_query, key_table, value_table, 0)
    far_part = call_cross_forward(infos[1], far_query, key_table, value_table, slots)
    other_part = swap(far_part, 2)
    place = me[None].astype(jnp.int32)
    out_tokens, grad_two, packed, vectors_mid, keep_mid, send_mid = call_middle(
        where, place, sum_one, own_part, other_part, vectors, live.astype(F32)[:, None],
        cotangent, tiles,
    )
    far_packed = swap(packed, 2)
    zeros = (jnp.zeros((D, D), F32), jnp.zeros((D, D), F32), jnp.zeros((8, D), F32))
    own_grad, *sums = call_cross_backward(
        infos[0], cross_query, packed, key_table, value_table, all_frames, zeros, 0
    )
    far_grad, grad_ck, grad_cv, bias_cv = call_cross_backward(
        infos[1], far_query, far_packed, key_table, value_table, all_frames, sums, slots
    )
    other_grad = swap(far_grad, 2)
    token_grads, vectors_last, keep_last, send_last = call_last(
        where, place, tokens, sum_one, grad_two, saved, own_grad, other_grad, vectors, layout, tiles
    )

    def split(grad):
        parts = (
            grad.astype(BF).reshape(4, 192, ROWS, PANEL).transpose(0, 2, 1, 3)
        )
        pieces = [lax.dynamic_index_in_dim(parts, me ^ i, 0, False) for i in range(4)]
        return jnp.stack([pieces[0], pieces[2]]), jnp.stack([pieces[1], pieces[3]])

    keep_k, send_k = split(grad_ck)
    keep_v, send_v = split(grad_cv)
    early = reduced(keep_mid, send_mid)
    late = reduced(
        jnp.concatenate([keep_k, keep_v, keep_last], axis=1),
        jnp.concatenate([send_k, send_v, send_last], axis=1),
    )
    at = {m: i for i, m in enumerate((7, *range(8, 16), 5, 6, 4, 3, 0, 1, 2))}
    spots = jnp.asarray([at[p // ROWS] * ROWS + p % ROWS for p in range(panel_total)], jnp.int32)
    slot_ids = group_index * cap + jnp.arange(cap, dtype=jnp.int32)
    matches = slot_of[:, None] == slot_ids[None, :]
    spot = jnp.sum(jnp.where(matches, spots[:, None], 0), axis=0, dtype=jnp.int32)
    used = jnp.any(matches, axis=0)[:, None, None]
    owned = jnp.concatenate([early, late], axis=0)[spot].transpose(0, 2, 1)
    grad_vectors = jnp.concatenate(
        [vectors_last[0:8], bias_cv[0:1], vectors_mid[0:10]], axis=0
    )
    vector_total = lax.psum(grad_vectors, ("dp", "frame"))
    grad_scale = 1.0 / math.sqrt(row_count * group_count * frame_count)
    matrix_grads = jnp.where(used, owned.astype(F32) * grad_scale, 0.0)
    matrix_first, matrix_second, matrix_weights = adam_update(
        matrix_grads, first_moment, second_moment, master, RATE_MATRIX, DECAY_MATRIX
    )
    matrix_first = jnp.where(used, matrix_first, 0.0)
    matrix_second = jnp.where(used, matrix_second, 0.0)
    matrix_weights = jnp.where(used, matrix_weights, 0.0)
    vector_grads = vector_total * grad_scale
    vector_first_new, vector_second_new, vector_weights = adam_update(
        vector_grads, vector_first, vector_second, vectors, RATE_VECTOR, 0.0
    )
    return (
        out_tokens,
        token_grads,
        matrix_grads,
        matrix_first,
        matrix_second,
        matrix_weights,
        vector_grads,
        vector_first_new,
        vector_second_new,
        vector_weights,
    )


def solution(mesh):
    in_specs = (
        P(("dp", "frame"), None),
        P("dp", "frame", None),
        P(("dp", "frame"), None),
        P("dp"),
        P("dp"),
        P(),
        P("dp", None, "frame"),
        P("dp", None, "frame"),
        P("dp", None, "frame"),
        P(),
        P(),
        P(),
    )
    out_specs = (
        P(("dp", "frame"), None),
        P(("dp", "frame"), None),
        P("dp", None, "frame"),
        P("dp", None, "frame"),
        P("dp", None, "frame"),
        P("dp", None, "frame"),
        P(),
        P(),
        P(),
        P(),
    )
    return jax.shard_map(body, mesh=mesh, in_specs=in_specs, out_specs=out_specs, check_vma=False)
```

```python
import functools
import math

import jax
import jax.numpy as jnp
from jax import lax
from jax.experimental import pallas as pl
from jax.experimental.pallas import tpu as pltpu
from jax.sharding import PartitionSpec as P

D = 768
HEADS = 12
HEAD = 64
FF = 3072
BLOCK = 64
PANEL = 128
STEP = 4
WIDE = 256
GROUPS = D // WIDE
ROWS = 6
MATS = 16
PARTIAL = 544
PACKED = 560

EPS_NORM = 1e-05
EPS_ADAM = 1e-08
BETA_ONE = 0.5
BETA_TWO = 0.5
RATE_MATRIX = 0.04
RATE_VECTOR = 0.2
DECAY_MATRIX = 0.01
MASKED = -1e30
SCALE = HEAD**-0.5

BF = jnp.bfloat16
F32 = jnp.float32
VMEM_LIMIT = 60 * 1024 * 1024


def dot_nt(a, b):
    return lax.dot_general(a, b, (((1,), (1,)), ((), ())), preferred_element_type=F32)


def dot_nn(a, b):
    return lax.dot_general(a, b, (((1,), (0,)), ((), ())), preferred_element_type=F32)


def eye():
    return (
        lax.broadcasted_iota(jnp.int32, (WIDE, WIDE), 0)
        == lax.broadcasted_iota(jnp.int32, (WIDE, WIDE), 1)
    ).astype(BF)


def turned(x, unit):
    parts = [
        dot_nt(unit, x[:, s : s + WIDE]).astype(BF) for s in range(0, x.shape[1], WIDE)
    ]
    return parts[0] if len(parts) == 1 else jnp.concatenate(parts, axis=0)


def head_mask():
    return (
        lax.broadcasted_iota(jnp.int32, (WIDE, WIDE), 0) >> 6
        == lax.broadcasted_iota(jnp.int32, (WIDE, WIDE), 1) >> 6
    )


def row_pick():
    return (
        lax.broadcasted_iota(jnp.int32, (HEAD, WIDE), 0)
        == lax.broadcasted_iota(jnp.int32, (HEAD, WIDE), 1) & (HEAD - 1)
    ).astype(BF)


def thirds(x):
    high = x.astype(BF)
    rest = x - high.astype(F32)
    middle = rest.astype(BF)
    return high, middle, (rest - middle.astype(F32)).astype(BF)


def norm_parts(v):
    average = jnp.mean(v, axis=-1, keepdims=True)
    centred = v - average
    inverse = lax.rsqrt(jnp.mean(centred * centred, axis=-1, keepdims=True) + EPS_NORM)
    return centred * inverse, inverse


def norm_back(e, unit_rows, inverse, gain):
    f = e * gain
    lean = jnp.mean(f, axis=-1, keepdims=True)
    slant = jnp.mean(f * unit_rows, axis=-1, keepdims=True)
    return (f - lean - unit_rows * slant) * inverse


def column_sum(x):
    return jnp.sum(x, axis=0, keepdims=True)


def matrix_copies(tiles, where, matrix, target, sem):
    copies = []
    for r in range(ROWS):
        for f in range(4):
            copies.append(
                pltpu.make_async_copy(
                    tiles.at[where[(matrix * ROWS + r) * 4 + f]],
                    target.at[pl.ds(f * 192, 192), pl.ds(r * PANEL, PANEL)],
                    sem,
                )
            )
    return copies


def gradient_copies(staged, keep, send, slot, me, sem):
    copies = []
    for relative in range(4):
        f = relative ^ me
        target = send if relative & 1 else keep
        for r in range(ROWS):
            copies.append(
                pltpu.make_async_copy(
                    staged.at[pl.ds(pl.multiple_of(f * 192, 64), 192), pl.ds(r * PANEL, PANEL)],
                    target.at[relative >> 1, slot * ROWS + r],
                    sem,
                )
            )
    return copies


def start_all(copies):
    for copy in copies:
        copy.start()


def wait_all(copies):
    for copy in copies:
        copy.wait()


def seen_bias(count, member_column, live_column, member_row):
    key_ids = lax.broadcasted_iota(jnp.int32, (count, count), 0)
    row_ids = lax.broadcasted_iota(jnp.int32, (count, count), 1)
    seen = (
        (member_column[...] == member_row[...])
        & (key_ids <= row_ids)
        & ((live_column[...] > 0) | (key_ids == row_ids))
    )
    return jnp.where(seen, 0.0, MASKED)


def front_kernel(
    where, tokens, vectors, member_column, live_column, member_row, tiles,
    sum_one, cross_query, query, key, value, attended, lse,
    weights, bias, sems,
):
    loads = [
        matrix_copies(tiles, where, i, weights.at[i], sems.at[i]) for i in range(5)
    ]
    for load in loads:
        start_all(load)
    unit = eye()
    count = tokens.shape[0]
    bias[...] = seen_bias(count, member_column, live_column, member_row)
    x = tokens[...].astype(F32)
    a = (norm_parts(x)[0] * vectors[0:1] + vectors[1:2]).astype(BF)
    wait_all(loads[0])
    query[...] = (SCALE * (dot_nt(a, weights[0]) + vectors[2:3])).astype(BF)
    wait_all(loads[1])
    key[...] = dot_nt(a, weights[1]).astype(BF)
    wait_all(loads[2])
    value[...] = (dot_nt(a, weights[2]) + vectors[3:4]).astype(BF)
    lanes = lax.broadcasted_iota(jnp.int32, (1, WIDE), 1) >> 6
    lse[...] = jnp.zeros_like(lse)
    for g in range(GROUPS):
        cols = pl.ds(g * WIDE, WIDE)
        q, k = query[:, cols], key[:, cols]
        v_turned = turned(value[:, cols], unit)
        outs = []
        for h in range(4):
            masked_q = jnp.where(lanes == h, q, jnp.zeros_like(q))
            scores = dot_nt(k, masked_q) + bias[...]
            top = jnp.max(scores, axis=0, keepdims=True)
            p = jnp.exp(scores - top)
            total = jnp.sum(p, axis=0, keepdims=True)
            out = dot_nn(v_turned[h * HEAD : (h + 1) * HEAD], p.astype(BF))
            outs.append((out * (1.0 / total)).astype(BF))
            lse[g * 4 + h : g * 4 + h + 1] = top + jnp.log(total)
        attended[:, cols] = turned(jnp.concatenate(outs, axis=0), unit)
    wait_all(loads[3])
    h1 = x + (dot_nt(attended[...], weights[3]) + vectors[4:5])
    sum_one[...] = h1
    c = (norm_parts(h1)[0] * vectors[5:6] + vectors[6:7]).astype(BF)
    wait_all(loads[4])
    cross_query[...] = (SCALE * (dot_nt(c, weights[4]) + vectors[7:8])).astype(BF)


def tables_kernel(act, where, frames, vectors, tiles, key_table, value_table, weights, sems):
    step = pl.program_id(0)

    @pl.when(step == 0)
    def _():
        loads = [
            matrix_copies(tiles, where, 5 + i, weights.at[i], sems.at[i]) for i in range(2)
        ]
        for load in loads:
            start_all(load)
        for load in loads:
            wait_all(load)

    @pl.when(step < act[0])
    def _():
        f = frames[0]
        key_table[0] = dot_nt(f, weights[0]).astype(BF)
        value_table[0] = (dot_nt(f, weights[1]) + vectors[8:9]).astype(BF)


def pad_rows(scores, fill):
    half = scores.shape[0] // 2
    odd = lax.broadcasted_iota(jnp.int32, (16, 1), 0) + (half - 16) >= 375
    parts = []
    for s in (0, half):
        parts.append(scores[s : s + half - 16])
        parts.append(jnp.where(odd, fill, scores[s + half - 16 : s + half]))
    return jnp.concatenate(parts, axis=0)


def each_unit(info, body):
    step = pl.program_id(0)
    first, mine = info[10 + step], info[18 + step]
    rest = jnp.where(step == 0, 8 - info[1], 0)

    def one(j, state):
        body(jnp.where(j < mine, first + j, info[1] + j - mine))
        return state

    lax.fori_loop(0, mine + rest, one, 0)


def spread_heads(x, mask):
    return jnp.where(mask, jnp.concatenate([x] * 4, axis=0), jnp.zeros((), x.dtype))


def cross_forward_kernel(info, query, key_table, value_table, out, value_turned, lse):
    step = pl.program_id(0)

    @pl.when(step < info[0])
    def _():
        unit, mask, pick = eye(), head_mask(), row_pick()
        for g in range(GROUPS):
            cols = pl.ds(g * WIDE, WIDE)
            value_turned[g] = turned(value_table[0, :, cols], unit)

        def body(u):
            rows = pl.ds(pl.multiple_of(u * BLOCK, BLOCK), BLOCK)
            for g in range(GROUPS):
                cols = pl.ds(g * WIDE, WIDE)
                wide_q = spread_heads(query[rows, cols], mask)
                scores = pad_rows(dot_nt(key_table[0, :, cols], wide_q), MASKED)
                top = jnp.max(scores, axis=0, keepdims=True)
                p = jnp.exp(scores - top)
                total = jnp.sum(p, axis=0, keepdims=True)
                o = dot_nn(value_turned[g], p.astype(BF)) * (1.0 / total)
                o = jnp.where(mask, o, 0.0).astype(BF)
                out[rows, cols] = dot_nt(pick, o).astype(BF)
                lse[pl.ds(u, 1), cols] = top + jnp.log(total)

        each_unit(info, body)

    @pl.when(step == pl.num_programs(0) - 1)
    def _():
        parts = [t.astype(F32) for t in thirds(lse[...])]
        parts.append(jnp.zeros_like(parts[0]))
        out[512:PARTIAL] = jnp.concatenate(parts, axis=0).astype(BF)


def cross_backward_kernel(
    info, query, packed, key_table, value_table, earlier, also_earlier,
    grad_query, key_out, value_out, bias_grad,
    key_turned, key_sum, value_sum, lse, delta,
):
    step = pl.program_id(0)

    @pl.when(step == 0)
    def _():
        bias_grad[...] = jnp.zeros_like(bias_grad)
        extra = packed[512:PACKED].astype(F32)
        lse[...] = extra[0:8] + extra[8:16] + extra[16:24]
        delta[...] = extra[24:32] + extra[32:40] + extra[40:48]

    @pl.when(step < info[0])
    def _():
        unit, mask, pick = eye(), head_mask(), row_pick()
        for g in range(GROUPS):
            cols = pl.ds(g * WIDE, WIDE)
            key_turned[g] = turned(key_table[0, :, cols], unit)
        key_sum[...] = jnp.zeros_like(key_sum)
        value_sum[...] = jnp.zeros_like(value_sum)

        def body(u):
            rows = pl.ds(pl.multiple_of(u * BLOCK, BLOCK), BLOCK)
            for g in range(GROUPS):
                cols = pl.ds(g * WIDE, WIDE)
                wide_q = spread_heads(query[rows, cols], mask)
                wide_o = spread_heads(packed[rows, cols], mask)
                scores = dot_nt(key_table[0, :, cols], wide_q)
                p = pad_rows(jnp.exp(scores - lse[pl.ds(u, 1), cols]), 0.0)
                dp = dot_nt(value_table[0, :, cols], wide_o)
                ds = (p * (dp - delta[pl.ds(u, 1), cols])).astype(BF)
                value_sum[:, cols] += dot_nn(p.astype(BF), wide_o)
                key_sum[:, cols] += dot_nn(ds, wide_q)
                dq = jnp.where(mask, dot_nn(key_turned[g], ds), 0.0).astype(BF)
                grad_query[rows, cols] = dot_nt(pick, dq).astype(BF)

        each_unit(info, body)
        for g in range(GROUPS):
            cols = pl.ds(g * WIDE, WIDE)
            low = value_sum[:, cols].astype(BF)
            bias_grad[0:1, cols] += column_sum(low.astype(F32))
            key_out[0, cols, :] = turned(key_sum[:, cols].astype(BF), unit)
            value_out[0, cols, :] = turned(low, unit)


def table_gradient_kernel(
    info_own, info_far, me, key_own, value_own, frames_own, key_far, value_far, frames_far,
    earlier,
    keep, send, grad_key, grad_value, staged, sem,
):
    step = pl.program_id(0)

    @pl.when(step == 0)
    def _():
        grad_key[...] = jnp.zeros_like(grad_key)
        grad_value[...] = jnp.zeros_like(grad_value)

    for info, key, value, frames in (
        (info_own, key_own, value_own, frames_own),
        (info_far, key_far, value_far, frames_far),
    ):

        @pl.when(step < info[0])
        def _():
            f = frames[0]
            grad_key[...] += dot_nn(key[0], f)
            grad_value[...] += dot_nn(value[0], f)

    @pl.when(step == pl.num_programs(0) - 1)
    def _():
        staged[0] = grad_key[...].astype(BF)
        staged[1] = grad_value[...].astype(BF)
        copies = [gradient_copies(staged.at[i], keep, send, i, me[0], sem) for i in range(2)]
        for copy in copies:
            start_all(copy)
        for copy in copies:
            wait_all(copy)


def middle_kernel(
    where, me, sum_one, own, other, vectors, live, cotangent, tiles,
    out_tokens, grad_two, packed, vector_grads, keep, send,
    weights, hidden, act, staged, third, merged, sems, out_sem,
):
    count = sum_one.shape[0]
    loads = {
        m: matrix_copies(tiles, where, m, weights.at[m - 7], sems.at[m - 7]) for m in range(7, 16)
    }
    for load in loads.values():
        start_all(load)
    unit, mask, pick = eye(), head_mask(), row_pick()
    lse_own = own[512:536].astype(F32)
    lse_other = other[512:536].astype(F32)
    lse_own = lse_own[0:8] + lse_own[8:16] + lse_own[16:24]
    lse_other = lse_other[0:8] + lse_other[8:16] + lse_other[16:24]
    top = jnp.maximum(lse_own, lse_other)
    weight_own = jnp.exp(lse_own - top)
    weight_other = jnp.exp(lse_other - top)
    total = weight_own + weight_other
    share = weight_own / total
    lse = top + jnp.log(total)
    for u in range(count // BLOCK):
        rows = pl.ds(u * BLOCK, BLOCK)
        for g in range(GROUPS):
            cols = pl.ds(g * WIDE, WIDE)
            part = share[u : u + 1, g * WIDE : (g + 1) * WIDE]
            high = part.astype(BF)
            low = (part - high.astype(F32)).astype(BF)
            none = jnp.zeros((), BF)
            factor = dot_nt(pick, jnp.where(mask, high, none)) + dot_nt(
                pick, jnp.where(mask, low, none)
            )
            first, second = own[rows, cols].astype(F32), other[rows, cols].astype(F32)
            merged[rows, cols] = second + factor * (first - second)
    cross_out = merged[...].astype(BF)
    wait_all(loads[7])
    h2 = sum_one[...] + (dot_nt(cross_out, weights[0]) + vectors[9:10])
    unit_three, inverse_three = norm_parts(h2)
    m = (unit_three * vectors[10:11] + vectors[11:12]).astype(BF)
    third[...] = h2 + vectors[16:17]
    for c in range(4):
        wait_all(loads[8 + c])
        wait_all(loads[12 + c])

    def ahead(c, state):
        u = dot_nt(m, weights[1 + c]) + vectors[pl.ds(12 + c, 1)]
        hidden[c] = u
        g = (u * (0.5 * (1.0 + lax.erf(u * math.sqrt(0.5))))).astype(BF)
        act[c] = g
        third[...] += dot_nt(g, weights[5 + c])
        return state

    lax.fori_loop(0, 4, ahead, 0)
    unit_last, inverse_last = norm_parts(third[...])
    alive = live[...]
    out_tokens[...] = (unit_last * vectors[17:18] + vectors[18:19]) * alive
    e = cotangent[...].astype(F32) * alive
    vector_grads[...] = jnp.zeros_like(vector_grads)
    vector_grads[8:9] = column_sum(e * unit_last)
    vector_grads[9:10] = column_sum(e)
    dh3 = norm_back(e, unit_last, inverse_last, vectors[17:18])
    third[...] = dh3
    e3 = dh3.astype(BF)
    vector_grads[7:8] = column_sum(e3.astype(F32))
    e3_turned = turned(e3, unit)
    grad_two[...] = jnp.zeros_like(grad_two)

    def back(c, state):
        staged[5 + c] = dot_nn(e3_turned, act[c]).astype(BF)
        start_all(gradient_copies(staged.at[5 + c], keep, send, 5 + c, me[0], out_sem))
        u = hidden[c]
        slope = 0.5 * (1.0 + lax.erf(u * math.sqrt(0.5))) + u * (
            jnp.exp(-0.5 * u * u) * (1.0 / math.sqrt(2.0 * math.pi))
        )
        du = (dot_nn(e3, weights[5 + c]) * slope).astype(BF)
        vector_grads[pl.ds(3 + c, 1)] = column_sum(du.astype(F32))
        staged[1 + c] = dot_nn(turned(du, unit), m).astype(BF)
        start_all(gradient_copies(staged.at[1 + c], keep, send, 1 + c, me[0], out_sem))
        grad_two[...] += dot_nn(du, weights[1 + c])
        return state

    lax.fori_loop(0, 4, back, 0)
    dm = grad_two[...]
    vector_grads[1:2] = column_sum(dm * unit_three)
    vector_grads[2:3] = column_sum(dm)
    dh2 = third[...] + norm_back(dm, unit_three, inverse_three, vectors[10:11])
    grad_two[...] = dh2
    e2 = dh2.astype(BF)
    vector_grads[0:1] = column_sum(e2.astype(F32))
    staged[0] = dot_nn(turned(e2, unit), cross_out).astype(BF)
    start_all(gradient_copies(staged.at[0], keep, send, 0, me[0], out_sem))
    packed[0:512] = dot_nn(e2, weights[0]).astype(BF)
    ones = jnp.ones((8, WIDE), BF)
    deltas = []
    for u in range(count // BLOCK):
        rows = pl.ds(u * BLOCK, BLOCK)
        line = []
        for g in range(GROUPS):
            cols = pl.ds(g * WIDE, WIDE)
            product = packed[rows, cols].astype(F32) * merged[rows, cols]
            high, middle, low = (spread_heads(t, mask) for t in thirds(product))
            line.append((dot_nt(ones, high) + dot_nt(ones, middle) + dot_nt(ones, low))[0:1])
        deltas.append(jnp.concatenate(line, axis=1))
    delta = jnp.concatenate(deltas, axis=0)
    extra = [t.astype(F32) for t in thirds(lse)] + [t.astype(F32) for t in thirds(delta)]
    packed[512:PACKED] = jnp.concatenate(extra, axis=0).astype(BF)
    for i in range(9):
        wait_all(gradient_copies(staged.at[i], keep, send, i, me[0], out_sem))


def cross_back_kernel(
    where, me, sum_one, grad_two, attended, own, other, vectors, tiles, earlier, also_earlier,
    grad_one, grad_att, vector_grads, keep, send,
    weights, staged, sems, out_sem,
):
    loads = [matrix_copies(tiles, where, m, weights.at[i], sems.at[i]) for i, m in enumerate((4, 3))]
    for load in loads:
        start_all(load)
    unit = eye()

    def put(slot, grad):
        staged[slot] = grad.astype(BF)
        start_all(gradient_copies(staged.at[slot], keep, send, slot, me[0], out_sem))

    ecq = (own[...].astype(F32) + other[...].astype(F32)).astype(BF) * jnp.asarray(SCALE, BF)
    vector_grads[...] = jnp.zeros_like(vector_grads)
    vector_grads[3:4] = column_sum(ecq.astype(F32))
    unit_two, inverse_two = norm_parts(sum_one[...])
    c = (unit_two * vectors[5:6] + vectors[6:7]).astype(BF)
    put(0, dot_nn(turned(ecq, unit), c))
    wait_all(loads[0])
    dc = dot_nn(ecq, weights[0])
    vector_grads[1:2] = column_sum(dc * unit_two)
    vector_grads[2:3] = column_sum(dc)
    dh1 = grad_two[...] + norm_back(dc, unit_two, inverse_two, vectors[5:6])
    grad_one[...] = dh1
    e1 = dh1.astype(BF)
    vector_grads[0:1] = column_sum(e1.astype(F32))
    put(1, dot_nn(turned(e1, unit), attended[...]))
    wait_all(loads[1])
    grad_att[...] = dot_nn(e1, weights[1]).astype(BF)
    for i in range(2):
        wait_all(gradient_copies(staged.at[i], keep, send, i, me[0], out_sem))


def last_kernel(
    where, me, tokens, grad_one, grad_att, query, key, value, lse, vectors,
    member_column, live_column, member_row, tiles, earlier,
    token_grads, vector_grads, keep, send,
    weights, staged, bias, grad_q, grad_q_turned, grad_k, grad_v, sems, out_sem,
):
    loads = [matrix_copies(tiles, where, i, weights.at[i], sems.at[i]) for i in range(3)]
    for load in loads:
        start_all(load)
    unit = eye()
    count = tokens.shape[0]
    bias[...] = seen_bias(count, member_column, live_column, member_row)

    def put(slot, grad):
        staged[slot] = grad.astype(BF)
        start_all(gradient_copies(staged.at[slot], keep, send, slot, me[0], out_sem))

    lanes = lax.broadcasted_iota(jnp.int32, (1, WIDE), 1) >> 6
    for g in range(GROUPS):
        cols = pl.ds(g * WIDE, WIDE)
        q, k, v, do = query[:, cols], key[:, cols], value[:, cols], grad_att[:, cols]
        k_turned = turned(k, unit)
        dk = jnp.zeros((count, WIDE), F32)
        dv = jnp.zeros((count, WIDE), F32)
        for h in range(4):
            none = jnp.zeros_like(q)
            masked_q = jnp.where(lanes == h, q, none)
            masked_o = jnp.where(lanes == h, do, none)
            scores = dot_nt(k, masked_q) + bias[...]
            p = jnp.exp(scores - lse[g * 4 + h : g * 4 + h + 1])
            dp = dot_nt(v, masked_o)
            drift = jnp.sum(p * dp, axis=0, keepdims=True)
            ds = (p * (dp - drift)).astype(BF)
            dv = dv + dot_nn(p.astype(BF), masked_o)
            dk = dk + dot_nn(ds, masked_q)
            dq = dot_nn(k_turned[h * HEAD : (h + 1) * HEAD], ds).astype(BF)
            spot = g * WIDE + h * HEAD
            grad_q_turned[spot : spot + HEAD] = dq * jnp.asarray(SCALE, BF)
        grad_k[:, cols] = dk.astype(BF)
        grad_v[:, cols] = dv.astype(BF)
        grad_q[:, cols] = turned(grad_q_turned[cols, :], unit)
    x = tokens[...].astype(F32)
    unit_one, inverse_one = norm_parts(x)
    a = (unit_one * vectors[0:1] + vectors[1:2]).astype(BF)
    vector_grads[...] = jnp.zeros_like(vector_grads)
    vector_grads[2:3] = column_sum(grad_q[...].astype(F32))
    vector_grads[3:4] = column_sum(grad_v[...].astype(F32))
    put(0, dot_nn(grad_q_turned[...], a))
    put(1, dot_nn(turned(grad_k[...], unit), a))
    put(2, dot_nn(turned(grad_v[...], unit), a))
    for load in loads:
        wait_all(load)
    da = (
        dot_nn(grad_q[...], weights[0])
        + dot_nn(grad_k[...], weights[1])
        + dot_nn(grad_v[...], weights[2])
    )
    vector_grads[0:1] = column_sum(da * unit_one)
    vector_grads[1:2] = column_sum(da)
    token_grads[...] = grad_one[...] + norm_back(da, unit_one, inverse_one, vectors[0:1])
    for i in range(3):
        wait_all(gradient_copies(staged.at[i], keep, send, i, me[0], out_sem))


def panel_copies(place, early, late, target, sem):
    cap = target.shape[0]
    count = early.shape[0] // 192

    def rows(i):
        return pl.ds(pl.multiple_of(i * 192, 192), 192)

    def start(i, state):
        @pl.when(place[i] < count)
        def _():
            pltpu.make_async_copy(early.at[rows(place[i])], target.at[i], sem).start()

        @pl.when(place[i] >= count)
        def _():
            pltpu.make_async_copy(late.at[rows(place[i] - count)], target.at[i], sem).start()

        return state

    def wait(i, state):
        pltpu.make_async_copy(early.at[pl.ds(0, 192)], target.at[i], sem).wait()
        return state

    lax.fori_loop(0, cap, start, 0)
    lax.fori_loop(0, cap, wait, 0)


def pick_kernel(place, early, late, earlier, out, sem):
    del earlier
    panel_copies(place, early, late, out, sem)


def update_kernel_of(
    row_total, place, source, early, late, got, master, first_moment, second_moment,
    grad_out, first_out, second_out, weight_out, own, sem,
):
    cap = got.shape[0]
    panel_copies(place, early, late, own, sem)

    def one(i, state):
        used = source[i] < 2
        low = jnp.where(source[i] == 0, own[i], got[i])
        grad = jnp.where(used, low.astype(F32) * (1.0 / math.sqrt(row_total)), 0.0)
        first, second, weight = adam_update(
            grad, first_moment[i], second_moment[i], master[i], RATE_MATRIX, DECAY_MATRIX
        )
        grad_out[i] = grad
        first_out[i] = jnp.where(used, first, 0.0)
        second_out[i] = jnp.where(used, second, 0.0)
        weight_out[i] = jnp.where(used, weight, 0.0)
        return state

    lax.fori_loop(0, cap, one, 0)


SMEM = pl.BlockSpec(memory_space=pltpu.SMEM)
WHOLE = pl.BlockSpec(memory_space=pltpu.VMEM)
AWAY = pl.BlockSpec(memory_space=pl.ANY)
PARAMS = pltpu.CompilerParams(vmem_limit_bytes=VMEM_LIMIT)


def cost(microseconds):
    return pl.CostEstimate(
        flops=int(microseconds * 1e9), bytes_accessed=1 << 20, transcendentals=0
    )


def shape(*dims, dtype=BF):
    return jax.ShapeDtypeStruct(dims, dtype)


def call_front(where, tokens, vectors, layout, tiles):
    count = tokens.shape[0]
    return pl.pallas_call(
        front_kernel,
        out_shape=(
            shape(count, D, dtype=F32),
            *(shape(count, D) for _ in range(5)),
            shape(16, count, dtype=F32),
        ),
        in_specs=[SMEM, WHOLE, WHOLE, WHOLE, WHOLE, WHOLE, AWAY],
        out_specs=(WHOLE,) * 7,
        scratch_shapes=[
            pltpu.VMEM((5, D, D), BF),
            pltpu.VMEM((count, count), F32),
            pltpu.SemaphoreType.DMA((5,)),
        ],
        compiler_params=PARAMS,
        cost_estimate=cost(16),
        name="front",
    )(where, tokens, vectors, *layout, tiles)


def call_tables(act, where, frames, vectors, tiles):
    slots, extent, _ = frames.shape

    def place(i, act, where):
        return (act[1 + i], 0, 0)

    block = pl.BlockSpec((1, extent, D), place)
    return pl.pallas_call(
        tables_kernel,
        out_shape=(shape(slots, extent, D),) * 2,
        grid_spec=pltpu.PrefetchScalarGridSpec(
            num_scalar_prefetch=2,
            grid=(slots,),
            in_specs=[block, WHOLE, AWAY],
            out_specs=(block, block),
            scratch_shapes=[pltpu.VMEM((2, D, D), BF), pltpu.SemaphoreType.DMA((2,))],
        ),
        compiler_params=PARAMS,
        cost_estimate=cost(30),
        name="tables",
    )(act, where, frames, vectors, tiles)


def whole_spec(*dims):
    return pl.BlockSpec(dims, lambda i, info: (0,) * len(dims))


def call_cross_forward(info, query, key_table, value_table, base):
    count, extent = query.shape[0], key_table.shape[1]
    slots = 8
    block = pl.BlockSpec((1, extent, D), lambda i, info: (base + info[2 + i], 0, 0))
    return pl.pallas_call(
        cross_forward_kernel,
        out_shape=shape(PARTIAL, D),
        grid_spec=pltpu.PrefetchScalarGridSpec(
            num_scalar_prefetch=1,
            grid=(slots,),
            in_specs=[whole_spec(count, D), block, block],
            out_specs=whole_spec(PARTIAL, D),
            scratch_shapes=[
                pltpu.VMEM((GROUPS, WIDE, extent), BF),
                pltpu.VMEM((8, D), F32),
            ],
        ),
        compiler_params=PARAMS,
        cost_estimate=cost(23),
        name="cross_forward",
    )(info, query, key_table, value_table)


def call_cross_backward(info, query, packed, key_table, value_table, earlier, base):
    count, extent = query.shape[0], key_table.shape[1]
    slots = 8
    block = pl.BlockSpec((1, extent, D), lambda i, info: (base + info[2 + i], 0, 0))
    block_out = pl.BlockSpec((1, D, extent), lambda i, info: (info[2 + i], 0, 0))
    return pl.pallas_call(
        cross_backward_kernel,
        out_shape=(
            shape(count, D),
            shape(slots, D, extent),
            shape(slots, D, extent),
            shape(8, D, dtype=F32),
        ),
        grid_spec=pltpu.PrefetchScalarGridSpec(
            num_scalar_prefetch=1,
            grid=(slots,),
            in_specs=[whole_spec(count, D), whole_spec(PACKED, D), block, block, AWAY, AWAY],
            out_specs=(whole_spec(count, D), block_out, block_out, whole_spec(8, D)),
            scratch_shapes=[
                pltpu.VMEM((GROUPS, WIDE, extent), BF),
                pltpu.VMEM((extent, D), F32),
                pltpu.VMEM((extent, D), F32),
                pltpu.VMEM((8, D), F32),
                pltpu.VMEM((8, D), F32),
            ],
        ),
        compiler_params=PARAMS,
        cost_estimate=cost(40),
        name="cross_backward",
    )(info, query, packed, key_table, value_table, *earlier)


def call_table_gradient(infos, me, own, far, frames, earlier):
    slots, extent = own[0].shape[0], frames.shape[1]

    def block(part, base, *dims):
        return pl.BlockSpec((1, *dims), lambda i, *infos: (base + infos[part][2 + i], 0, 0))

    specs = []
    for part in range(2):
        specs += [block(part, 0, D, extent)] * 2 + [block(part, part * slots, extent, D)]
    part = shape(2, 2 * ROWS, 192, PANEL)
    return pl.pallas_call(
        table_gradient_kernel,
        out_shape=(part, part),
        grid_spec=pltpu.PrefetchScalarGridSpec(
            num_scalar_prefetch=3,
            grid=(slots,),
            in_specs=[*specs, AWAY],
            out_specs=(AWAY, AWAY),
            scratch_shapes=[
                pltpu.VMEM((D, D), F32),
                pltpu.VMEM((D, D), F32),
                pltpu.VMEM((2, D, D), BF),
                pltpu.SemaphoreType.DMA,
            ],
        ),
        compiler_params=PARAMS,
        cost_estimate=cost(20),
        name="table_gradient",
    )(*infos, me, *own, frames, *far, frames, earlier)


def call_middle(where, me, sum_one, own, other, vectors, live, cotangent, tiles):
    count = sum_one.shape[0]
    part = shape(2, 9 * ROWS, 192, PANEL)
    return pl.pallas_call(
        middle_kernel,
        out_shape=(
            shape(count, D, dtype=F32),
            shape(count, D, dtype=F32),
            shape(PACKED, D),
            shape(16, D, dtype=F32),
            part,
            part,
        ),
        in_specs=[SMEM, SMEM, WHOLE, WHOLE, WHOLE, WHOLE, WHOLE, WHOLE, AWAY],
        out_specs=(WHOLE, WHOLE, WHOLE, WHOLE, AWAY, AWAY),
        scratch_shapes=[
            pltpu.VMEM((9, D, D), BF),
            pltpu.VMEM((4, count, D), F32),
            pltpu.VMEM((4, count, D), BF),
            pltpu.VMEM((9, D, D), BF),
            pltpu.VMEM((count, D), F32),
            pltpu.VMEM((count, D), F32),
            pltpu.SemaphoreType.DMA((9,)),
            pltpu.SemaphoreType.DMA,
        ],
        compiler_params=PARAMS,
        cost_estimate=cost(34),
        name="middle",
    )(where, me, sum_one, own, other, vectors, live, cotangent, tiles)


def call_cross_back(where, me, sum_one, grad_two, attended, own, other, vectors, tiles, earlier):
    count = sum_one.shape[0]
    part = shape(2, 2 * ROWS, 192, PANEL)
    return pl.pallas_call(
        cross_back_kernel,
        out_shape=(shape(count, D, dtype=F32), shape(count, D), shape(8, D, dtype=F32), part, part),
        in_specs=[SMEM, SMEM] + [WHOLE] * 6 + [AWAY] * 3,
        out_specs=(WHOLE, WHOLE, WHOLE, AWAY, AWAY),
        scratch_shapes=[
            pltpu.VMEM((2, D, D), BF),
            pltpu.VMEM((2, D, D), BF),
            pltpu.SemaphoreType.DMA((2,)),
            pltpu.SemaphoreType.DMA,
        ],
        compiler_params=PARAMS,
        cost_estimate=cost(8),
        name="cross_back",
    )(where, me, sum_one, grad_two, attended, own, other, vectors, tiles, *earlier)


def call_last(where, me, tokens, grad_one, grad_att, saved, vectors, layout, tiles, earlier):
    count = tokens.shape[0]
    part = shape(2, 3 * ROWS, 192, PANEL)
    return pl.pallas_call(
        last_kernel,
        out_shape=(shape(count, D, dtype=F32), shape(8, D, dtype=F32), part, part),
        in_specs=[SMEM, SMEM] + [WHOLE] * 11 + [AWAY] * 2,
        out_specs=(WHOLE, WHOLE, AWAY, AWAY),
        scratch_shapes=[
            pltpu.VMEM((3, D, D), BF),
            pltpu.VMEM((3, D, D), BF),
            pltpu.VMEM((count, count), F32),
            pltpu.VMEM((count, D), BF),
            pltpu.VMEM((D, count), BF),
            pltpu.VMEM((count, D), BF),
            pltpu.VMEM((count, D), BF),
            pltpu.SemaphoreType.DMA((3,)),
            pltpu.SemaphoreType.DMA,
        ],
        compiler_params=PARAMS,
        cost_estimate=cost(20),
        name="last",
    )(where, me, tokens, grad_one, grad_att, *saved, vectors, *layout, tiles, earlier)


def call_pick(place, early, late, earlier):
    cap = place.shape[0]
    return pl.pallas_call(
        pick_kernel,
        out_shape=shape(cap, 192, PANEL),
        in_specs=[SMEM, AWAY, AWAY, AWAY],
        out_specs=WHOLE,
        scratch_shapes=[pltpu.SemaphoreType.DMA],
        compiler_params=PARAMS,
        cost_estimate=cost(3),
        name="pick",
    )(place, early, late, earlier)


def call_update(row_total, place, source, early, late, got, weights):
    cap = got.shape[0]
    return pl.pallas_call(
        functools.partial(update_kernel_of, row_total),
        out_shape=(shape(cap, 192, PANEL, dtype=F32),) * 4,
        in_specs=[SMEM, SMEM, AWAY, AWAY] + [WHOLE] * 4,
        out_specs=(WHOLE,) * 4,
        scratch_shapes=[pltpu.VMEM((cap, 192, PANEL), BF), pltpu.SemaphoreType.DMA],
        compiler_params=PARAMS,
        cost_estimate=cost(6),
        name="update",
    )(place, source, early, late, got, *weights)


def row_layout(bucket, length, row_count):
    starts = jnp.cumsum(bucket, dtype=jnp.int32) - bucket
    row_ids = jnp.arange(row_count, dtype=jnp.int32)
    slot_ids = jnp.arange(bucket.shape[0], dtype=jnp.int32)
    block_ids = row_ids // BLOCK
    inside = (block_ids[:, None] >= starts[None, :]) & (
        block_ids[:, None] < (starts + bucket)[None, :]
    )
    member = jnp.where(
        jnp.any(inside, axis=1),
        jnp.sum(jnp.where(inside, slot_ids[None, :], 0), axis=1, dtype=jnp.int32),
        -1,
    )
    live = jnp.any(
        inside & (row_ids[:, None] - BLOCK * starts[None, :] < length[None, :]), axis=1
    )
    return member, live


def packed_slots(bucket):
    count = bucket.shape[0]
    ids = jnp.arange(count, dtype=jnp.int32)
    taken = bucket > 0
    number = jnp.sum(taken, dtype=jnp.int32)
    rank = jnp.cumsum(taken, dtype=jnp.int32) - 1
    step = jnp.minimum(ids, number - 1)
    hit = (rank[None, :] == step[:, None]) & taken[None, :]

    def pick(values):
        return jnp.sum(jnp.where(hit, values[None, :], 0), axis=1, dtype=jnp.int32)

    starts = jnp.cumsum(bucket, dtype=jnp.int32) - bucket
    return number, pick(ids), pick(starts), pick(bucket)


def adam_update(gradient, first_moment, second_moment, weight, step_rate, decay_rate):
    first_new = BETA_ONE * first_moment + (1.0 - BETA_ONE) * gradient
    second_new = BETA_TWO * second_moment + (1.0 - BETA_TWO) * gradient * gradient
    fix_one = 1.0 - BETA_ONE**STEP
    fix_two = 1.0 - BETA_TWO**STEP
    update = first_new / fix_one / (jnp.sqrt(second_new / fix_two) + EPS_ADAM)
    return (first_new, second_new, weight - step_rate * (update + decay_rate * weight))


def swap(x, bit):
    return lax.ppermute(x, "frame", [(i, i ^ bit) for i in range(4)])


def over_dp(x, bit):
    size = lax.axis_size("dp")
    return lax.ppermute(x, "dp", [(i, i ^ bit) for i in range(size)])


def added(a, b):
    return (a.astype(F32) + b.astype(F32)).astype(BF)


def frame_sum(keep, send):
    mine = added(keep, swap(send, 1))
    return added(mine[0], swap(mine[1], 2))


def dp_bits():
    size, bits = lax.axis_size("dp"), []
    while 2 ** len(bits) < size:
        bits.append(2 ** len(bits))
    return bits


def half_sum(x, bit):
    half = x.shape[0] // 2
    upper = (lax.axis_index("dp") // bit) & 1
    kept = lax.dynamic_slice_in_dim(x, upper * half, half)
    sent = lax.dynamic_slice_in_dim(x, (1 - upper) * half, half)
    return added(kept, over_dp(sent, bit))


def both_halves(x, bit):
    upper = (lax.axis_index("dp") // bit) & 1
    got = over_dp(x, bit)
    return jnp.where(
        upper == 0, jnp.concatenate([x, got], axis=0), jnp.concatenate([got, x], axis=0)
    )


def total_sum(x):
    for bit in (1, 2):
        x = x + swap(x, bit)
    for bit in dp_bits():
        x = x + over_dp(x, bit)
    return x


def body(
    tokens, frames, cotangent, buckets, lengths, slot_of, master, first_moment, second_moment,
    vectors, vector_first, vector_second,
):
    row_count = tokens.shape[0]
    group_count = lax.axis_size("dp")
    frame_count = lax.axis_size("frame")
    me = lax.axis_index("frame")
    group_index = lax.axis_index("dp")
    cap = master.shape[0]
    panel_total = slot_of.shape[0]
    slots = buckets.shape[0] // frame_count
    extent = frames.shape[1]

    tiles = lax.all_gather(
        master.astype(BF).transpose(0, 2, 1)[None], ("dp", "frame"), axis=0, tiled=True
    )
    tiles = tiles.reshape(group_count * frame_count * cap, master.shape[2], PANEL)
    quarter_ids = jnp.arange(frame_count, dtype=jnp.int32)
    where = (
        ((slot_of // cap)[:, None] * frame_count + quarter_ids[None, :]) * cap
        + (slot_of % cap)[:, None]
    ).reshape(-1)

    core, far = me & 1, me >> 1
    room = (extent + 15) // 16 * 16
    by_buffer = frames.reshape(2, 2, slots, extent, D)

    def halves(bit):
        part = lax.dynamic_index_in_dim(by_buffer, bit, 1, False)
        first = lax.dynamic_index_in_dim(part, far, 0, False)
        second = lax.dynamic_index_in_dim(part, 1 - far, 0, False)
        return jnp.pad(
            jnp.concatenate([first, second], axis=0), ((0, 0), (0, room - extent), (0, 0))
        )

    all_frames = jnp.concatenate([halves(core), swap(halves(1 - core), 1)], axis=1)

    by_device = buckets.reshape(frame_count, slots)
    own_bucket = lax.dynamic_index_in_dim(by_device, me, 0, False)
    far_bucket = lax.dynamic_index_in_dim(by_device, me ^ 2, 0, False)
    own_length = lax.dynamic_index_in_dim(lengths.reshape(frame_count, slots), me, 0, False)
    infos = []
    for bucket in (own_bucket, far_bucket):
        number, places, starts, units = packed_slots(bucket)
        infos.append(
            jnp.concatenate([jnp.stack([number, jnp.sum(bucket)]), places, starts, units])
        )
    both = packed_slots(jnp.concatenate([own_bucket, far_bucket]))
    act = jnp.concatenate([both[0][None], both[1]])
    member, live = row_layout(own_bucket, own_length, row_count)
    layout = (member[:, None], live.astype(jnp.int32)[:, None], member[None, :])

    key_table, value_table = call_tables(act, where, all_frames, vectors, tiles)
    sum_one, cross_query, *saved = call_front(where, tokens, vectors, layout, tiles)
    far_query = swap(cross_query, 2)
    own_part = call_cross_forward(infos[0], cross_query, key_table, value_table, 0)
    far_part = call_cross_forward(infos[1], far_query, key_table, value_table, slots)
    other_part = swap(far_part, 2)
    place = me[None].astype(jnp.int32)
    out_tokens, grad_two, packed, vectors_mid, keep_mid, send_mid = call_middle(
        where, place, sum_one, own_part, other_part, vectors, live.astype(F32)[:, None],
        cotangent, tiles,
    )
    far_packed = swap(packed, 2)
    pair_mid = added(keep_mid, swap(send_mid, 1))
    cuts = (0, 3 * ROWS, 9 * ROWS)

    def across(part):
        mine = pair_mid[:, cuts[part] : cuts[part + 1]]
        return added(mine[0], swap(mine[1], 2))

    own_grad, *own_sums, own_bias = call_cross_backward(
        infos[0], cross_query, packed, key_table, value_table, (pair_mid, pair_mid), 0
    )
    early_one = across(0)
    far_grad, *far_sums, far_bias = call_cross_backward(
        infos[1], far_query, far_packed, key_table, value_table, (own_grad, early_one), slots
    )
    early_two = across(1)
    early = jnp.concatenate([early_one, early_two], axis=0).reshape(-1, PANEL)
    bits = dp_bits()
    other_grad = swap(far_grad, 2)
    keep_table, send_table = call_table_gradient(
        infos, place, own_sums, far_sums, all_frames, early_two
    )
    *saved_heads, attended, lse = saved
    early = half_sum(early, bits[0])
    grad_one, grad_att, vectors_cross, keep_cross, send_cross = call_cross_back(
        where, place, sum_one, grad_two, attended, own_grad, other_grad, vectors, tiles,
        (keep_table, early),
    )
    early = half_sum(early, bits[1])
    pair_cross = added(
        jnp.concatenate([keep_table, keep_cross], axis=1),
        swap(jnp.concatenate([send_table, send_cross], axis=1), 1),
    )
    token_grads, vectors_last, keep_last, send_last = call_last(
        where, place, tokens, grad_one, grad_att, [*saved_heads, lse], vectors, layout, tiles,
        pair_cross,
    )
    late = jnp.concatenate(
        [added(pair_cross[0], swap(pair_cross[1], 2)), frame_sum(keep_last, send_last)], axis=0
    ).reshape(-1, PANEL)
    late = half_sum(late, bits[0])
    for bit in bits[2:]:
        early = half_sum(early, bit)
    for bit in bits[1:]:
        late = half_sum(late, bit)
    for bit in reversed(bits[1:]):
        early = both_halves(early, bit)
        late = both_halves(late, bit)
    grad_vectors = jnp.concatenate(
        [
            vectors_last[0:4],
            vectors_cross[0:4],
            own_bias[0:1] + far_bias[0:1],
            vectors_mid[0:10],
            jnp.zeros((5, D), F32),
        ],
        axis=0,
    )
    vector_total = total_sum(grad_vectors)[0 : vectors.shape[0]]
    held = ((7, *range(8, 16)), (5, 6, 4, 3, 0, 1, 2))
    halves_of, places_of = {}, {}
    base = 0
    for matrices in held:
        middle = len(matrices) * ROWS // 2
        for i in range(2 * middle):
            panel = matrices[i // ROWS] * ROWS + i % ROWS
            halves_of[panel] = i // middle
            places_of[panel] = base + i % middle
        base += middle
    panel_half = jnp.asarray([halves_of[p] for p in range(panel_total)], jnp.int32)
    panel_place = jnp.asarray([places_of[p] for p in range(panel_total)], jnp.int32)

    def slots_of(group):
        slot_ids = group * cap + jnp.arange(cap, dtype=jnp.int32)
        matches = slot_of[:, None] == slot_ids[None, :]
        half, place_ = (
            jnp.sum(jnp.where(matches, values[:, None], 0), axis=0, dtype=jnp.int32)
            for values in (panel_half, panel_place)
        )
        return half, place_, jnp.any(matches, axis=0)

    upper = (group_index // bits[0]) & 1
    half, own_place, used = slots_of(group_index)
    far_place = slots_of(group_index ^ bits[0])[1]
    got = over_dp(call_pick(far_place, early, late, vector_total), bits[0])
    row_total = row_count * group_count * frame_count
    updates = call_update(
        row_total,
        own_place,
        jnp.where(used, jnp.where(half == upper, 0, 1), 2),
        early,
        late,
        got,
        [w.transpose(0, 2, 1) for w in (master, first_moment, second_moment)],
    )
    matrix_grads, matrix_first, matrix_second, matrix_weights = (
        u.transpose(0, 2, 1) for u in updates
    )
    vector_grads = vector_total * (1.0 / math.sqrt(row_total))
    vector_first_new, vector_second_new, vector_weights = adam_update(
        vector_grads, vector_first, vector_second, vectors, RATE_VECTOR, 0.0
    )
    return (
        out_tokens,
        token_grads,
        matrix_grads,
        matrix_first,
        matrix_second,
        matrix_weights,
        vector_grads,
        vector_first_new,
        vector_second_new,
        vector_weights,
    )


def solution(mesh):
    in_specs = (
        P(("dp", "frame"), None),
        P("dp", "frame", None),
        P(("dp", "frame"), None),
        P("dp"),
        P("dp"),
        P(),
        P("dp", None, "frame"),
        P("dp", None, "frame"),
        P("dp", None, "frame"),
        P(),
        P(),
        P(),
    )
    out_specs = (
        P(("dp", "frame"), None),
        P(("dp", "frame"), None),
        P("dp", None, "frame"),
        P("dp", None, "frame"),
        P("dp", None, "frame"),
        P("dp", None, "frame"),
        P(),
        P(),
        P(),
        P(),
    )
    return jax.shard_map(body, mesh=mesh, in_specs=in_specs, out_specs=out_specs, check_vma=False)
```

```python
import functools
import math

import jax
import jax.numpy as jnp
from jax import lax
from jax.experimental import pallas as pl
from jax.experimental.pallas import tpu as pltpu
from jax.sharding import PartitionSpec as P

D = 768
HEADS = 12
HEAD = 64
FF = 3072
BLOCK = 64
PANEL = 128
STEP = 4
WIDE = 256
GROUPS = D // WIDE
ROWS = 6
MATS = 16
PARTIAL = 544
PACKED = 560

EPS_NORM = 1e-05
EPS_ADAM = 1e-08
BETA_ONE = 0.5
BETA_TWO = 0.5
RATE_MATRIX = 0.04
RATE_VECTOR = 0.2
DECAY_MATRIX = 0.01
MASKED = -1e30
SCALE = HEAD**-0.5

BF = jnp.bfloat16
F32 = jnp.float32
VMEM_LIMIT = 60 * 1024 * 1024


def dot_nt(a, b):
    return lax.dot_general(a, b, (((1,), (1,)), ((), ())), preferred_element_type=F32)


def dot_nn(a, b):
    return lax.dot_general(a, b, (((1,), (0,)), ((), ())), preferred_element_type=F32)


def dot_tn(a, b):
    return lax.dot_general(a, b, (((0,), (0,)), ((), ())), preferred_element_type=F32)


def eye():
    return (
        lax.broadcasted_iota(jnp.int32, (WIDE, WIDE), 0)
        == lax.broadcasted_iota(jnp.int32, (WIDE, WIDE), 1)
    ).astype(BF)


def turned(x, unit):
    parts = [
        dot_nt(unit, x[:, s : s + WIDE]).astype(BF) for s in range(0, x.shape[1], WIDE)
    ]
    return parts[0] if len(parts) == 1 else jnp.concatenate(parts, axis=0)


def head_mask():
    return (
        lax.broadcasted_iota(jnp.int32, (WIDE, WIDE), 0) >> 6
        == lax.broadcasted_iota(jnp.int32, (WIDE, WIDE), 1) >> 6
    )


def row_pick():
    return (
        lax.broadcasted_iota(jnp.int32, (HEAD, WIDE), 0)
        == lax.broadcasted_iota(jnp.int32, (HEAD, WIDE), 1) & (HEAD - 1)
    ).astype(BF)


def thirds(x):
    high = x.astype(BF)
    rest = x - high.astype(F32)
    middle = rest.astype(BF)
    return high, middle, (rest - middle.astype(F32)).astype(BF)


def norm_parts(v):
    average = jnp.mean(v, axis=-1, keepdims=True)
    centred = v - average
    inverse = lax.rsqrt(jnp.mean(centred * centred, axis=-1, keepdims=True) + EPS_NORM)
    return centred * inverse, inverse


def norm_back(e, unit_rows, inverse, gain):
    f = e * gain
    lean = jnp.mean(f, axis=-1, keepdims=True)
    slant = jnp.mean(f * unit_rows, axis=-1, keepdims=True)
    return (f - lean - unit_rows * slant) * inverse


def column_sum(x):
    return jnp.sum(x, axis=0, keepdims=True)


def matrix_start(tiles, where, matrix, target, sem):
    def start(source, base, r):
        for f in range(4):
            pltpu.make_async_copy(
                source.at[where[(matrix * ROWS + r) * 4 + f] - base],
                target.at[pl.ds(f * 192, 192), pl.ds(r * PANEL, PANEL)],
                sem,
            ).start()

    count = tiles[0].shape[0]
    for r in range(ROWS):
        if len(tiles) == 1:
            start(tiles[0], 0, r)
            continue
        near = where[(matrix * ROWS + r) * 4] < count
        pl.when(near)(functools.partial(start, tiles[0], 0, r))
        pl.when(jnp.logical_not(near))(functools.partial(start, tiles[1], count, r))


def matrix_wait(tiles, target, sem):
    for r in range(ROWS):
        for f in range(4):
            pltpu.make_async_copy(
                tiles[0].at[0],
                target.at[pl.ds(f * 192, 192), pl.ds(r * PANEL, PANEL)],
                sem,
            ).wait()


def gradient_copies(staged, keep, send, slot, me, sem):
    copies = []
    for relative in range(4):
        f = relative ^ me
        target = send if relative & 1 else keep
        for r in range(ROWS):
            copies.append(
                pltpu.make_async_copy(
                    staged.at[pl.ds(pl.multiple_of(f * 192, 64), 192), pl.ds(r * PANEL, PANEL)],
                    target.at[relative >> 1, slot * ROWS + r],
                    sem,
                )
            )
    return copies


def start_all(copies):
    for copy in copies:
        copy.start()


def wait_all(copies):
    for copy in copies:
        copy.wait()


def seen_bias(count, member_column, live_column, member_row):
    key_ids = lax.broadcasted_iota(jnp.int32, (count, count), 0)
    row_ids = lax.broadcasted_iota(jnp.int32, (count, count), 1)
    seen = (
        (member_column[...] == member_row[...])
        & (key_ids <= row_ids)
        & ((live_column[...] > 0) | (key_ids == row_ids))
    )
    return jnp.where(seen, 0.0, MASKED)


def front_kernel(
    where, tokens, vectors, member_column, live_column, member_row, tiles,
    sum_one, cross_query, query, key, value, attended, lse,
    weights, bias, sems,
):
    for i in range(5):
        matrix_start([tiles], where, i, weights.at[i], sems.at[i])
    unit = eye()
    count = tokens.shape[0]
    bias[...] = seen_bias(count, member_column, live_column, member_row)
    x = tokens[...].astype(F32)
    a = (norm_parts(x)[0] * vectors[0:1] + vectors[1:2]).astype(BF)
    matrix_wait([tiles], weights.at[0], sems.at[0])
    query[...] = (SCALE * (dot_nt(a, weights[0]) + vectors[2:3])).astype(BF)
    matrix_wait([tiles], weights.at[1], sems.at[1])
    key[...] = dot_nt(a, weights[1]).astype(BF)
    matrix_wait([tiles], weights.at[2], sems.at[2])
    value[...] = (dot_nt(a, weights[2]) + vectors[3:4]).astype(BF)
    lanes = lax.broadcasted_iota(jnp.int32, (1, WIDE), 1) >> 6
    lse[...] = jnp.zeros_like(lse)
    for g in range(GROUPS):
        cols = pl.ds(g * WIDE, WIDE)
        q, k = query[:, cols], key[:, cols]
        v_turned = turned(value[:, cols], unit)
        outs = []
        for h in range(4):
            masked_q = jnp.where(lanes == h, q, jnp.zeros_like(q))
            scores = dot_nt(k, masked_q) + bias[...]
            top = jnp.max(scores, axis=0, keepdims=True)
            p = jnp.exp(scores - top)
            total = jnp.sum(p, axis=0, keepdims=True)
            out = dot_nn(v_turned[h * HEAD : (h + 1) * HEAD], p.astype(BF))
            outs.append((out * (1.0 / total)).astype(BF))
            lse[g * 4 + h : g * 4 + h + 1] = top + jnp.log(total)
        attended[:, cols] = turned(jnp.concatenate(outs, axis=0), unit)
    matrix_wait([tiles], weights.at[3], sems.at[3])
    h1 = x + (dot_nt(attended[...], weights[3]) + vectors[4:5])
    sum_one[...] = h1
    c = (norm_parts(h1)[0] * vectors[5:6] + vectors[6:7]).astype(BF)
    matrix_wait([tiles], weights.at[4], sems.at[4])
    cross_query[...] = (SCALE * (dot_nt(c, weights[4]) + vectors[7:8])).astype(BF)


def tables_kernel(act, where, frames, vectors, tiles, key_table, value_table, weights, sems):
    step = pl.program_id(0)

    @pl.when(step == 0)
    def _():
        for i in range(2):
            matrix_start([tiles], where, 5 + i, weights.at[i], sems.at[i])
        for i in range(2):
            matrix_wait([tiles], weights.at[i], sems.at[i])

    @pl.when(step < act[0])
    def _():
        f = frames[0]
        key_table[0] = dot_nt(f, weights[0]).astype(BF)
        value_table[0] = (dot_nt(f, weights[1]) + vectors[8:9]).astype(BF)


def pad_rows(scores, fill):
    half = scores.shape[0] // 2
    odd = lax.broadcasted_iota(jnp.int32, (16, 1), 0) + (half - 16) >= 375
    parts = []
    for s in (0, half):
        parts.append(scores[s : s + half - 16])
        parts.append(jnp.where(odd, fill, scores[s + half - 16 : s + half]))
    return jnp.concatenate(parts, axis=0)


def units_of(info):
    step = pl.program_id(0)
    first, mine, used = info[10 + step], info[18 + step], info[1]
    rest = jnp.where(step == 0, 8 - used, 0)
    return first, (mine + rest - 1, lambda j: jnp.where(j + 1 < mine, first + j + 1, used + j + 1 - mine))


def each_unit(units, body):
    count, place = units

    def one(j, state):
        body(place(j))
        return state

    lax.fori_loop(0, count, one, 0)


def spread_heads(x, mask):
    return jnp.where(mask, jnp.concatenate([x] * 4, axis=0), jnp.zeros((), x.dtype))


def cross_forward_kernel(info, query, key_table, value_table, out, value_turned, lse):
    step = pl.program_id(0)

    @pl.when(step < info[0])
    def _():
        unit, mask, pick = eye(), head_mask(), row_pick()
        for g in range(GROUPS):
            cols = pl.ds(g * WIDE, WIDE)
            value_turned[g] = turned(value_table[0, :, cols], unit)

        def body(u):
            rows = pl.ds(pl.multiple_of(u * BLOCK, BLOCK), BLOCK)
            for g in range(GROUPS):
                cols = pl.ds(g * WIDE, WIDE)
                wide_q = spread_heads(query[rows, cols], mask)
                scores = pad_rows(dot_nt(key_table[0, :, cols], wide_q), MASKED)
                top = jnp.max(scores, axis=0, keepdims=True)
                p = jnp.exp(scores - top)
                total = jnp.sum(p, axis=0, keepdims=True)
                o = dot_nn(value_turned[g], p.astype(BF)) * (1.0 / total)
                o = jnp.where(mask, o, 0.0).astype(BF)
                out[rows, cols] = dot_nt(pick, o).astype(BF)
                lse[pl.ds(u, 1), cols] = top + jnp.log(total)

        first, others = units_of(info)
        body(first)
        each_unit(others, body)

    @pl.when(step == pl.num_programs(0) - 1)
    def _():
        parts = [t.astype(F32) for t in thirds(lse[...])]
        parts.append(jnp.zeros_like(parts[0]))
        out[512:PARTIAL] = jnp.concatenate(parts, axis=0).astype(BF)


def cross_backward_kernel(
    info, query, packed, key_table, value_table, earlier, also_earlier,
    grad_query, key_out, value_out, bias_grad,
    key_turned, key_sum, value_sum, lse, delta,
):
    step = pl.program_id(0)

    @pl.when(step == 0)
    def _():
        bias_grad[...] = jnp.zeros_like(bias_grad)
        extra = packed[512:PACKED].astype(F32)
        lse[...] = extra[0:8] + extra[8:16] + extra[16:24]
        delta[...] = extra[24:32] + extra[32:40] + extra[40:48]

    @pl.when(step < info[0])
    def _():
        unit, mask, pick = eye(), head_mask(), row_pick()
        for g in range(GROUPS):
            cols = pl.ds(g * WIDE, WIDE)
            key_turned[g] = turned(key_table[0, :, cols], unit)

        def body(u, first):
            rows = pl.ds(pl.multiple_of(u * BLOCK, BLOCK), BLOCK)
            for g in range(GROUPS):
                cols = pl.ds(g * WIDE, WIDE)
                wide_q = spread_heads(query[rows, cols], mask)
                wide_o = spread_heads(packed[rows, cols], mask)
                scores = dot_nt(key_table[0, :, cols], wide_q)
                p = pad_rows(jnp.exp(scores - lse[pl.ds(u, 1), cols]), 0.0)
                dp = dot_nt(value_table[0, :, cols], wide_o)
                ds = (p * (dp - delta[pl.ds(u, 1), cols])).astype(BF)
                part = dot_nn(p.astype(BF), wide_o)
                value_sum[:, cols] = part if first else value_sum[:, cols] + part
                part = dot_nn(ds, wide_q)
                key_sum[:, cols] = part if first else key_sum[:, cols] + part
                dq = jnp.where(mask, dot_nn(key_turned[g], ds), 0.0).astype(BF)
                grad_query[rows, cols] = dot_nt(pick, dq).astype(BF)

        first, others = units_of(info)
        body(first, True)
        each_unit(others, lambda u: body(u, False))
        ones = jnp.ones((8, key_sum.shape[0]), BF)
        for g in range(GROUPS):
            cols = pl.ds(g * WIDE, WIDE)
            low = value_sum[:, cols].astype(BF)
            bias_grad[:, cols] += dot_nn(ones, low)
            key_out[0, :, cols] = key_sum[:, cols].astype(BF)
            value_out[0, :, cols] = low


def table_gradient_kernel(
    info_own, info_far, me, key_own, value_own, frames_own, key_far, value_far, frames_far,
    earlier,
    keep, send, grad_key, grad_value, staged, sem,
):
    step = pl.program_id(0)

    @pl.when(step == 0)
    def _():
        grad_key[...] = jnp.zeros_like(grad_key)
        grad_value[...] = jnp.zeros_like(grad_value)

    for info, key, value, frames in (
        (info_own, key_own, value_own, frames_own),
        (info_far, key_far, value_far, frames_far),
    ):

        @pl.when(step < info[0])
        def _():
            f = frames[0]
            grad_key[...] += dot_tn(key[0], f)
            grad_value[...] += dot_tn(value[0], f)

    @pl.when(step == pl.num_programs(0) - 1)
    def _():
        staged[0] = grad_key[...].astype(BF)
        staged[1] = grad_value[...].astype(BF)
        copies = [gradient_copies(staged.at[i], keep, send, i, me[0], sem) for i in range(2)]
        for copy in copies:
            start_all(copy)
        for copy in copies:
            wait_all(copy)


def middle_kernel(
    part_count, where, me, sum_one, own, other, vectors, live, cotangent, *refs,
):
    tiles, refs = refs[:part_count], refs[part_count:]
    middle_rows(where, me, sum_one, own, other, vectors, live, cotangent, tiles, *refs)


def middle_rows(
    where, me, sum_one, own, other, vectors, live, cotangent, tiles,
    out_tokens, grad_two, packed, vector_grads, keep, send,
    weights, slope, act, staged, third, merged, sems, out_sem,
):
    count = sum_one.shape[0]
    for m in range(9):
        matrix_start(tiles, where, 7 + m, weights.at[m], sems.at[m])
    unit, mask, pick = eye(), head_mask(), row_pick()
    lse_own = own[512:536].astype(F32)
    lse_other = other[512:536].astype(F32)
    lse_own = lse_own[0:8] + lse_own[8:16] + lse_own[16:24]
    lse_other = lse_other[0:8] + lse_other[8:16] + lse_other[16:24]
    top = jnp.maximum(lse_own, lse_other)
    weight_own = jnp.exp(lse_own - top)
    weight_other = jnp.exp(lse_other - top)
    total = weight_own + weight_other
    share = weight_own / total
    lse = top + jnp.log(total)
    for u in range(count // BLOCK):
        rows = pl.ds(u * BLOCK, BLOCK)
        for g in range(GROUPS):
            cols = pl.ds(g * WIDE, WIDE)
            part = share[u : u + 1, g * WIDE : (g + 1) * WIDE]
            high = part.astype(BF)
            low = (part - high.astype(F32)).astype(BF)
            none = jnp.zeros((), BF)
            factor = dot_nt(pick, jnp.where(mask, high, none)) + dot_nt(
                pick, jnp.where(mask, low, none)
            )
            first, second = own[rows, cols].astype(F32), other[rows, cols].astype(F32)
            merged[rows, cols] = second + factor * (first - second)
    cross_out = merged[...].astype(BF)
    matrix_wait(tiles, weights.at[0], sems.at[0])
    h2 = sum_one[...] + (dot_nt(cross_out, weights[0]) + vectors[9:10])
    unit_three, inverse_three = norm_parts(h2)
    m = (unit_three * vectors[10:11] + vectors[11:12]).astype(BF)
    third[...] = h2 + vectors[16:17]
    for c in range(4):
        matrix_wait(tiles, weights.at[1 + c], sems.at[1 + c])
        matrix_wait(tiles, weights.at[5 + c], sems.at[5 + c])

    def ahead(c, state):
        u = dot_nt(m, weights[1 + c]) + vectors[pl.ds(12 + c, 1)]
        below = 0.5 * (1.0 + lax.erf(u * math.sqrt(0.5)))
        slope[c] = below + u * (jnp.exp(-0.5 * u * u) * (1.0 / math.sqrt(2.0 * math.pi)))
        g = (u * below).astype(BF)
        act[c] = g
        third[...] += dot_nt(g, weights[5 + c])
        return state

    lax.fori_loop(0, 4, ahead, 0)
    unit_last, inverse_last = norm_parts(third[...])
    alive = live[...]
    out_tokens[...] = (unit_last * vectors[17:18] + vectors[18:19]) * alive
    e = cotangent[...].astype(F32) * alive
    vector_grads[...] = jnp.zeros_like(vector_grads)
    vector_grads[8:9] = column_sum(e * unit_last)
    vector_grads[9:10] = column_sum(e)
    dh3 = norm_back(e, unit_last, inverse_last, vectors[17:18])
    third[...] = dh3
    e3 = dh3.astype(BF)
    vector_grads[7:8] = column_sum(e3.astype(F32))
    grad_two[...] = jnp.zeros_like(grad_two)

    def back(c, state):
        staged[5 + c] = dot_tn(e3, act[c]).astype(BF)
        start_all(gradient_copies(staged.at[5 + c], keep, send, 5 + c, me[0], out_sem))
        du = (dot_nn(e3, weights[5 + c]) * slope[c]).astype(BF)
        vector_grads[pl.ds(3 + c, 1)] = column_sum(du.astype(F32))
        staged[1 + c] = dot_tn(du, m).astype(BF)
        start_all(gradient_copies(staged.at[1 + c], keep, send, 1 + c, me[0], out_sem))
        grad_two[...] += dot_nn(du, weights[1 + c])
        return state

    lax.fori_loop(0, 4, back, 0)
    dm = grad_two[...]
    vector_grads[1:2] = column_sum(dm * unit_three)
    vector_grads[2:3] = column_sum(dm)
    dh2 = third[...] + norm_back(dm, unit_three, inverse_three, vectors[10:11])
    grad_two[...] = dh2
    e2 = dh2.astype(BF)
    vector_grads[0:1] = column_sum(e2.astype(F32))
    staged[0] = dot_tn(e2, cross_out).astype(BF)
    start_all(gradient_copies(staged.at[0], keep, send, 0, me[0], out_sem))
    packed[0:512] = dot_nn(e2, weights[0]).astype(BF)
    ones = jnp.ones((8, WIDE), BF)
    deltas = []
    for u in range(count // BLOCK):
        rows = pl.ds(u * BLOCK, BLOCK)
        line = []
        for g in range(GROUPS):
            cols = pl.ds(g * WIDE, WIDE)
            product = packed[rows, cols].astype(F32) * merged[rows, cols]
            high, middle, low = (spread_heads(t, mask) for t in thirds(product))
            line.append((dot_nt(ones, high) + dot_nt(ones, middle) + dot_nt(ones, low))[0:1])
        deltas.append(jnp.concatenate(line, axis=1))
    delta = jnp.concatenate(deltas, axis=0)
    extra = [t.astype(F32) for t in thirds(lse)] + [t.astype(F32) for t in thirds(delta)]
    packed[512:PACKED] = jnp.concatenate(extra, axis=0).astype(BF)
    for i in range(9):
        wait_all(gradient_copies(staged.at[i], keep, send, i, me[0], out_sem))


def cross_back_kernel(
    part_count, where, me, sum_one, grad_two, attended, own, other, vectors, earlier, also_earlier, *refs,
):
    tiles, refs = refs[:part_count], refs[part_count:]
    cross_back_rows(where, me, sum_one, grad_two, attended, own, other, vectors, tiles, *refs)


def cross_back_rows(
    where, me, sum_one, grad_two, attended, own, other, vectors, tiles,
    grad_one, grad_att, vector_grads, keep, send,
    weights, staged, sems, out_sem,
):
    for i, m in enumerate((4, 3)):
        matrix_start(tiles, where, m, weights.at[i], sems.at[i])
    unit = eye()

    def put(slot, grad):
        staged[slot] = grad.astype(BF)
        start_all(gradient_copies(staged.at[slot], keep, send, slot, me[0], out_sem))

    ecq = (own[...].astype(F32) + other[...].astype(F32)).astype(BF) * jnp.asarray(SCALE, BF)
    vector_grads[...] = jnp.zeros_like(vector_grads)
    vector_grads[3:4] = column_sum(ecq.astype(F32))
    unit_two, inverse_two = norm_parts(sum_one[...])
    c = (unit_two * vectors[5:6] + vectors[6:7]).astype(BF)
    put(0, dot_tn(ecq, c))
    matrix_wait(tiles, weights.at[0], sems.at[0])
    dc = dot_nn(ecq, weights[0])
    vector_grads[1:2] = column_sum(dc * unit_two)
    vector_grads[2:3] = column_sum(dc)
    dh1 = grad_two[...] + norm_back(dc, unit_two, inverse_two, vectors[5:6])
    grad_one[...] = dh1
    e1 = dh1.astype(BF)
    vector_grads[0:1] = column_sum(e1.astype(F32))
    put(1, dot_tn(e1, attended[...]))
    matrix_wait(tiles, weights.at[1], sems.at[1])
    grad_att[...] = dot_nn(e1, weights[1]).astype(BF)
    for i in range(2):
        wait_all(gradient_copies(staged.at[i], keep, send, i, me[0], out_sem))


def last_kernel(
    part_count, where, me, tokens, grad_one, grad_att, query, key, value, lse, vectors,
    member_column, live_column, member_row, earlier, *refs,
):
    tiles, refs = refs[:part_count], refs[part_count:]
    last_rows(
        where, me, tokens, grad_one, grad_att, query, key, value, lse, vectors,
        member_column, live_column, member_row, tiles, *refs,
    )


def last_rows(
    where, me, tokens, grad_one, grad_att, query, key, value, lse, vectors,
    member_column, live_column, member_row, tiles,
    token_grads, vector_grads, keep, send,
    weights, staged, bias, grad_q, grad_q_turned, grad_k, grad_v, sems, out_sem,
):
    for i in range(3):
        matrix_start(tiles, where, i, weights.at[i], sems.at[i])
    unit = eye()
    count = tokens.shape[0]
    bias[...] = seen_bias(count, member_column, live_column, member_row)

    def put(slot, grad):
        staged[slot] = grad.astype(BF)
        start_all(gradient_copies(staged.at[slot], keep, send, slot, me[0], out_sem))

    lanes = lax.broadcasted_iota(jnp.int32, (1, WIDE), 1) >> 6
    for g in range(GROUPS):
        cols = pl.ds(g * WIDE, WIDE)
        q, k, v, do = query[:, cols], key[:, cols], value[:, cols], grad_att[:, cols]
        k_turned = turned(k, unit)
        dk = jnp.zeros((count, WIDE), F32)
        dv = jnp.zeros((count, WIDE), F32)
        for h in range(4):
            none = jnp.zeros_like(q)
            masked_q = jnp.where(lanes == h, q, none)
            masked_o = jnp.where(lanes == h, do, none)
            scores = dot_nt(k, masked_q) + bias[...]
            p = jnp.exp(scores - lse[g * 4 + h : g * 4 + h + 1])
            dp = dot_nt(v, masked_o)
            drift = jnp.sum(p * dp, axis=0, keepdims=True)
            ds = (p * (dp - drift)).astype(BF)
            dv = dv + dot_nn(p.astype(BF), masked_o)
            dk = dk + dot_nn(ds, masked_q)
            dq = dot_nn(k_turned[h * HEAD : (h + 1) * HEAD], ds).astype(BF)
            spot = g * WIDE + h * HEAD
            grad_q_turned[spot : spot + HEAD] = dq * jnp.asarray(SCALE, BF)
        grad_k[:, cols] = dk.astype(BF)
        grad_v[:, cols] = dv.astype(BF)
        grad_q[:, cols] = turned(grad_q_turned[cols, :], unit)
    x = tokens[...].astype(F32)
    unit_one, inverse_one = norm_parts(x)
    a = (unit_one * vectors[0:1] + vectors[1:2]).astype(BF)
    vector_grads[...] = jnp.zeros_like(vector_grads)
    vector_grads[2:3] = column_sum(grad_q[...].astype(F32))
    vector_grads[3:4] = column_sum(grad_v[...].astype(F32))
    put(0, dot_nn(grad_q_turned[...], a))
    put(1, dot_tn(grad_k[...], a))
    put(2, dot_tn(grad_v[...], a))
    for i in range(3):
        matrix_wait(tiles, weights.at[i], sems.at[i])
    da = (
        dot_nn(grad_q[...], weights[0])
        + dot_nn(grad_k[...], weights[1])
        + dot_nn(grad_v[...], weights[2])
    )
    vector_grads[0:1] = column_sum(da * unit_one)
    vector_grads[1:2] = column_sum(da)
    token_grads[...] = grad_one[...] + norm_back(da, unit_one, inverse_one, vectors[0:1])
    for i in range(3):
        wait_all(gradient_copies(staged.at[i], keep, send, i, me[0], out_sem))


def panel_copies(place, early, late, target, sem):
    cap = target.shape[0]
    count = early.shape[0] // 192

    def rows(i):
        return pl.ds(pl.multiple_of(i * 192, 192), 192)

    def start(i, state):
        @pl.when(place[i] < count)
        def _():
            pltpu.make_async_copy(early.at[rows(place[i])], target.at[i], sem).start()

        @pl.when(place[i] >= count)
        def _():
            pltpu.make_async_copy(late.at[rows(place[i] - count)], target.at[i], sem).start()

        return state

    def wait(i, state):
        pltpu.make_async_copy(early.at[pl.ds(0, 192)], target.at[i], sem).wait()
        return state

    lax.fori_loop(0, cap, start, 0)
    lax.fori_loop(0, cap, wait, 0)


def pick_kernel(place, early, late, earlier, out, sem):
    del earlier
    panel_copies(place, early, late, out, sem)


def update_kernel_of(
    row_total, place, source, early, late, got, master, first_moment, second_moment,
    grad_out, first_out, second_out, weight_out, own, sem,
):
    cap = got.shape[0]
    panel_copies(place, early, late, own, sem)

    def one(i, state):
        used = source[i] < 2
        low = jnp.where(source[i] == 0, own[i], got[i])
        grad = jnp.where(used, low.astype(F32) * (1.0 / math.sqrt(row_total)), 0.0)
        first, second, weight = adam_update(
            grad, first_moment[i], second_moment[i], master[i], RATE_MATRIX, DECAY_MATRIX
        )
        grad_out[i] = grad
        first_out[i] = jnp.where(used, first, 0.0)
        second_out[i] = jnp.where(used, second, 0.0)
        weight_out[i] = jnp.where(used, weight, 0.0)
        return state

    lax.fori_loop(0, cap, one, 0)


SMEM = pl.BlockSpec(memory_space=pltpu.SMEM)
WHOLE = pl.BlockSpec(memory_space=pltpu.VMEM)
AWAY = pl.BlockSpec(memory_space=pl.ANY)
PARAMS = pltpu.CompilerParams(vmem_limit_bytes=VMEM_LIMIT)


def cost(microseconds):
    return pl.CostEstimate(
        flops=int(microseconds * 1e9), bytes_accessed=1 << 20, transcendentals=0
    )


def shape(*dims, dtype=BF):
    return jax.ShapeDtypeStruct(dims, dtype)


def call_front(where, tokens, vectors, layout, tiles):
    count = tokens.shape[0]
    return pl.pallas_call(
        front_kernel,
        out_shape=(
            shape(count, D, dtype=F32),
            *(shape(count, D) for _ in range(5)),
            shape(16, count, dtype=F32),
        ),
        in_specs=[SMEM, WHOLE, WHOLE, WHOLE, WHOLE, WHOLE, AWAY],
        out_specs=(WHOLE,) * 7,
        scratch_shapes=[
            pltpu.VMEM((5, D, D), BF),
            pltpu.VMEM((count, count), F32),
            pltpu.SemaphoreType.DMA((5,)),
        ],
        compiler_params=PARAMS,
        cost_estimate=cost(16),
        name="front",
    )(where, tokens, vectors, *layout, tiles)


def call_tables(act, where, frames, vectors, tiles):
    slots, extent, _ = frames.shape

    def place(i, act, where):
        return (act[1 + i], 0, 0)

    block = pl.BlockSpec((1, extent, D), place)
    return pl.pallas_call(
        tables_kernel,
        out_shape=(shape(slots, extent, D),) * 2,
        grid_spec=pltpu.PrefetchScalarGridSpec(
            num_scalar_prefetch=2,
            grid=(slots,),
            in_specs=[block, WHOLE, AWAY],
            out_specs=(block, block),
            scratch_shapes=[pltpu.VMEM((2, D, D), BF), pltpu.SemaphoreType.DMA((2,))],
        ),
        compiler_params=PARAMS,
        cost_estimate=cost(30),
        name="tables",
    )(act, where, frames, vectors, tiles)


def whole_spec(*dims):
    return pl.BlockSpec(dims, lambda i, info: (0,) * len(dims))


def call_cross_forward(info, query, key_table, value_table, base):
    count, extent = query.shape[0], key_table.shape[1]
    slots = 8
    block = pl.BlockSpec((1, extent, D), lambda i, info: (base + info[2 + i], 0, 0))
    return pl.pallas_call(
        cross_forward_kernel,
        out_shape=shape(PARTIAL, D),
        grid_spec=pltpu.PrefetchScalarGridSpec(
            num_scalar_prefetch=1,
            grid=(slots,),
            in_specs=[whole_spec(count, D), block, block],
            out_specs=whole_spec(PARTIAL, D),
            scratch_shapes=[
                pltpu.VMEM((GROUPS, WIDE, extent), BF),
                pltpu.VMEM((8, D), F32),
            ],
        ),
        compiler_params=PARAMS,
        cost_estimate=cost(23),
        name="cross_forward",
    )(info, query, key_table, value_table)


def call_cross_backward(info, query, packed, key_table, value_table, earlier, base):
    count, extent = query.shape[0], key_table.shape[1]
    slots = 8
    block = pl.BlockSpec((1, extent, D), lambda i, info: (base + info[2 + i], 0, 0))
    block_out = pl.BlockSpec((1, extent, D), lambda i, info: (info[2 + i], 0, 0))
    return pl.pallas_call(
        cross_backward_kernel,
        out_shape=(
            shape(count, D),
            shape(slots, extent, D),
            shape(slots, extent, D),
            shape(8, D, dtype=F32),
        ),
        grid_spec=pltpu.PrefetchScalarGridSpec(
            num_scalar_prefetch=1,
            grid=(slots,),
            in_specs=[whole_spec(count, D), whole_spec(PACKED, D), block, block, AWAY, AWAY],
            out_specs=(whole_spec(count, D), block_out, block_out, whole_spec(8, D)),
            scratch_shapes=[
                pltpu.VMEM((GROUPS, WIDE, extent), BF),
                pltpu.VMEM((extent, D), F32),
                pltpu.VMEM((extent, D), F32),
                pltpu.VMEM((8, D), F32),
                pltpu.VMEM((8, D), F32),
            ],
        ),
        compiler_params=PARAMS,
        cost_estimate=cost(40),
        name="cross_backward",
    )(info, query, packed, key_table, value_table, *earlier)


def call_table_gradient(infos, me, own, far, frames, earlier):
    slots, extent = own[0].shape[0], frames.shape[1]

    def block(part, base, *dims):
        return pl.BlockSpec((1, *dims), lambda i, *infos: (base + infos[part][2 + i], 0, 0))

    specs = []
    for part in range(2):
        specs += [block(part, 0, extent, D)] * 2 + [block(part, part * slots, extent, D)]
    part = shape(2, 2 * ROWS, 192, PANEL)
    return pl.pallas_call(
        table_gradient_kernel,
        out_shape=(part, part),
        grid_spec=pltpu.PrefetchScalarGridSpec(
            num_scalar_prefetch=3,
            grid=(slots,),
            in_specs=[*specs, AWAY],
            out_specs=(AWAY, AWAY),
            scratch_shapes=[
                pltpu.VMEM((D, D), F32),
                pltpu.VMEM((D, D), F32),
                pltpu.VMEM((2, D, D), BF),
                pltpu.SemaphoreType.DMA,
            ],
        ),
        compiler_params=PARAMS,
        cost_estimate=cost(20),
        name="table_gradient",
    )(*infos, me, *own, frames, *far, frames, earlier)


def call_middle(where, me, sum_one, own, other, vectors, live, cotangent, tiles):
    count = sum_one.shape[0]
    part = shape(2, 9 * ROWS, 192, PANEL)
    return pl.pallas_call(
        functools.partial(middle_kernel, len(tiles)),
        out_shape=(
            shape(count, D, dtype=F32),
            shape(count, D, dtype=F32),
            shape(PACKED, D),
            shape(16, D, dtype=F32),
            part,
            part,
        ),
        in_specs=[SMEM, SMEM] + [WHOLE] * 6 + [AWAY] * len(tiles),
        out_specs=(WHOLE, WHOLE, WHOLE, WHOLE, AWAY, AWAY),
        scratch_shapes=[
            pltpu.VMEM((9, D, D), BF),
            pltpu.VMEM((4, count, D), F32),
            pltpu.VMEM((4, count, D), BF),
            pltpu.VMEM((9, D, D), BF),
            pltpu.VMEM((count, D), F32),
            pltpu.VMEM((count, D), F32),
            pltpu.SemaphoreType.DMA((9,)),
            pltpu.SemaphoreType.DMA,
        ],
        compiler_params=PARAMS,
        cost_estimate=cost(34),
        name="middle",
    )(where, me, sum_one, own, other, vectors, live, cotangent, *tiles)


def call_cross_back(where, me, sum_one, grad_two, attended, own, other, vectors, tiles, earlier):
    count = sum_one.shape[0]
    part = shape(2, 2 * ROWS, 192, PANEL)
    return pl.pallas_call(
        functools.partial(cross_back_kernel, len(tiles)),
        out_shape=(shape(count, D, dtype=F32), shape(count, D), shape(8, D, dtype=F32), part, part),
        in_specs=[SMEM, SMEM] + [WHOLE] * 6 + [AWAY] * (2 + len(tiles)),
        out_specs=(WHOLE, WHOLE, WHOLE, AWAY, AWAY),
        scratch_shapes=[
            pltpu.VMEM((2, D, D), BF),
            pltpu.VMEM((2, D, D), BF),
            pltpu.SemaphoreType.DMA((2,)),
            pltpu.SemaphoreType.DMA,
        ],
        compiler_params=PARAMS,
        cost_estimate=cost(8),
        name="cross_back",
    )(where, me, sum_one, grad_two, attended, own, other, vectors, *earlier, *tiles)


def call_last(where, me, tokens, grad_one, grad_att, saved, vectors, layout, tiles, earlier):
    count = tokens.shape[0]
    part = shape(2, 3 * ROWS, 192, PANEL)
    return pl.pallas_call(
        functools.partial(last_kernel, len(tiles)),
        out_shape=(shape(count, D, dtype=F32), shape(8, D, dtype=F32), part, part),
        in_specs=[SMEM, SMEM] + [WHOLE] * 11 + [AWAY] * (1 + len(tiles)),
        out_specs=(WHOLE, WHOLE, AWAY, AWAY),
        scratch_shapes=[
            pltpu.VMEM((3, D, D), BF),
            pltpu.VMEM((3, D, D), BF),
            pltpu.VMEM((count, count), F32),
            pltpu.VMEM((count, D), BF),
            pltpu.VMEM((D, count), BF),
            pltpu.VMEM((count, D), BF),
            pltpu.VMEM((count, D), BF),
            pltpu.SemaphoreType.DMA((3,)),
            pltpu.SemaphoreType.DMA,
        ],
        compiler_params=PARAMS,
        cost_estimate=cost(20),
        name="last",
    )(where, me, tokens, grad_one, grad_att, *saved, vectors, *layout, earlier, *tiles)


def call_pick(place, early, late, earlier):
    cap = place.shape[0]
    return pl.pallas_call(
        pick_kernel,
        out_shape=shape(cap, 192, PANEL),
        in_specs=[SMEM, AWAY, AWAY, AWAY],
        out_specs=WHOLE,
        scratch_shapes=[pltpu.SemaphoreType.DMA],
        compiler_params=PARAMS,
        cost_estimate=cost(3),
        name="pick",
    )(place, early, late, earlier)


def call_update(row_total, place, source, early, late, got, weights):
    cap = got.shape[0]
    return pl.pallas_call(
        functools.partial(update_kernel_of, row_total),
        out_shape=(shape(cap, 192, PANEL, dtype=F32),) * 4,
        in_specs=[SMEM, SMEM, AWAY, AWAY] + [WHOLE] * 4,
        out_specs=(WHOLE,) * 4,
        scratch_shapes=[pltpu.VMEM((cap, 192, PANEL), BF), pltpu.SemaphoreType.DMA],
        compiler_params=PARAMS,
        cost_estimate=cost(6),
        name="update",
    )(place, source, early, late, got, *weights)


def row_layout(bucket, length, row_count):
    starts = jnp.cumsum(bucket, dtype=jnp.int32) - bucket
    row_ids = jnp.arange(row_count, dtype=jnp.int32)
    slot_ids = jnp.arange(bucket.shape[0], dtype=jnp.int32)
    block_ids = row_ids // BLOCK
    inside = (block_ids[:, None] >= starts[None, :]) & (
        block_ids[:, None] < (starts + bucket)[None, :]
    )
    member = jnp.where(
        jnp.any(inside, axis=1),
        jnp.sum(jnp.where(inside, slot_ids[None, :], 0), axis=1, dtype=jnp.int32),
        -1,
    )
    live = jnp.any(
        inside & (row_ids[:, None] - BLOCK * starts[None, :] < length[None, :]), axis=1
    )
    return member, live


def packed_slots(bucket):
    count = bucket.shape[0]
    ids = jnp.arange(count, dtype=jnp.int32)
    taken = bucket > 0
    number = jnp.sum(taken, dtype=jnp.int32)
    rank = jnp.cumsum(taken, dtype=jnp.int32) - 1
    step = jnp.minimum(ids, number - 1)
    hit = (rank[None, :] == step[:, None]) & taken[None, :]

    def pick(values):
        return jnp.sum(jnp.where(hit, values[None, :], 0), axis=1, dtype=jnp.int32)

    starts = jnp.cumsum(bucket, dtype=jnp.int32) - bucket
    return number, pick(ids), pick(starts), pick(bucket)


def adam_update(gradient, first_moment, second_moment, weight, step_rate, decay_rate):
    first_new = BETA_ONE * first_moment + (1.0 - BETA_ONE) * gradient
    second_new = BETA_TWO * second_moment + (1.0 - BETA_TWO) * gradient * gradient
    fix_one = 1.0 - BETA_ONE**STEP
    fix_two = 1.0 - BETA_TWO**STEP
    update = first_new / fix_one / (jnp.sqrt(second_new / fix_two) + EPS_ADAM)
    return (first_new, second_new, weight - step_rate * (update + decay_rate * weight))


def swap(x, bit):
    return lax.ppermute(x, "frame", [(i, i ^ bit) for i in range(4)])


def over_dp(x, bit):
    size = lax.axis_size("dp")
    return lax.ppermute(x, "dp", [(i, i ^ bit) for i in range(size)])


def added(a, b):
    return (a.astype(F32) + b.astype(F32)).astype(BF)


def frame_sum(keep, send):
    mine = added(keep, swap(send, 1))
    return added(mine[0], swap(mine[1], 2))


def dp_bits():
    size, bits = lax.axis_size("dp"), []
    while 2 ** len(bits) < size:
        bits.append(2 ** len(bits))
    return bits


def half_sum(x, bit):
    half = x.shape[0] // 2
    upper = (lax.axis_index("dp") // bit) & 1
    kept = lax.dynamic_slice_in_dim(x, upper * half, half)
    sent = lax.dynamic_slice_in_dim(x, (1 - upper) * half, half)
    return added(kept, over_dp(sent, bit))


def both_halves(x, bit):
    upper = (lax.axis_index("dp") // bit) & 1
    got = over_dp(x, bit)
    return jnp.where(
        upper == 0, jnp.concatenate([x, got], axis=0), jnp.concatenate([got, x], axis=0)
    )


def total_sum(x):
    for bit in (1, 2):
        x = x + swap(x, bit)
    for bit in dp_bits():
        x = x + over_dp(x, bit)
    return x


CAP, FIRST = 16, 10
NEEDED = (5, 6, 0, 1, 2, 3, 4, *range(7, 16))
SOON = 7 * ROWS


def body(*args):
    slot_of, master = args[5], args[6]
    cap = master.shape[0]
    owner = slot_of // cap
    need = [NEEDED.index(p // ROWS) * ROWS + p % ROWS for p in range(slot_of.shape[0])]
    need = jnp.asarray(need, jnp.int32)
    rank = jnp.sum(
        (owner[:, None] == owner[None, :]) & (need[None, :] < need[:, None]), axis=1, dtype=jnp.int32
    )
    here = (owner == lax.axis_index("dp"))[None, :] & (
        rank[None, :] == jnp.arange(cap, dtype=jnp.int32)[:, None]
    )
    order = jnp.sum(jnp.where(here, (slot_of % cap)[None, :], 0), axis=1, dtype=jnp.int32)
    ordered = master.transpose(0, 2, 1)[order].astype(BF)
    if cap != CAP:
        return steps(cap, owner, rank, ordered, *args)
    soon = jnp.max(jnp.where(need < SOON, rank, 0)) < FIRST
    return lax.cond(
        soon,
        functools.partial(steps, FIRST),
        functools.partial(steps, cap),
        owner, rank, ordered, *args,
    )


def steps(
    first, owner, rank, ordered,
    tokens, frames, cotangent, buckets, lengths, slot_of, master, first_moment, second_moment,
    vectors, vector_first, vector_second,
):
    row_count = tokens.shape[0]
    group_count = lax.axis_size("dp")
    frame_count = lax.axis_size("frame")
    me = lax.axis_index("frame")
    group_index = lax.axis_index("dp")
    cap = master.shape[0]
    panel_total = slot_of.shape[0]
    slots = buckets.shape[0] // frame_count
    extent = frames.shape[1]

    def gathered(part):
        whole = lax.all_gather(part[None], ("dp", "frame"), axis=0, tiled=True)
        return whole.reshape(-1, *part.shape[1:])

    cuts = (0, first, cap) if first < cap else (0, cap)
    tiles = [gathered(ordered[a:b]) for a, b in zip(cuts, cuts[1:])]
    device = owner[:, None] * frame_count + jnp.arange(frame_count, dtype=jnp.int32)[None, :]
    place_of = rank[:, None]
    where = jnp.where(
        place_of < first,
        device * first + place_of,
        group_count * frame_count * first + device * (cap - first) + place_of - first,
    ).reshape(-1)

    core, far = me & 1, me >> 1
    room = (extent + 15) // 16 * 16
    by_buffer = frames.reshape(2, 2, slots, extent, D)

    def halves(bit):
        part = lax.dynamic_index_in_dim(by_buffer, bit, 1, False)
        first = lax.dynamic_index_in_dim(part, far, 0, False)
        second = lax.dynamic_index_in_dim(part, 1 - far, 0, False)
        return jnp.pad(
            jnp.concatenate([first, second], axis=0), ((0, 0), (0, room - extent), (0, 0))
        )

    all_frames = jnp.concatenate([halves(core), swap(halves(1 - core), 1)], axis=1)

    by_device = buckets.reshape(frame_count, slots)
    own_bucket = lax.dynamic_index_in_dim(by_device, me, 0, False)
    far_bucket = lax.dynamic_index_in_dim(by_device, me ^ 2, 0, False)
    own_length = lax.dynamic_index_in_dim(lengths.reshape(frame_count, slots), me, 0, False)
    infos = []
    for bucket in (own_bucket, far_bucket):
        number, places, starts, units = packed_slots(bucket)
        infos.append(
            jnp.concatenate([jnp.stack([number, jnp.sum(bucket)]), places, starts, units])
        )
    both = packed_slots(jnp.concatenate([own_bucket, far_bucket]))
    act = jnp.concatenate([both[0][None], both[1]])
    member, live = row_layout(own_bucket, own_length, row_count)
    layout = (member[:, None], live.astype(jnp.int32)[:, None], member[None, :])

    key_table, value_table = call_tables(act, where, all_frames, vectors, tiles[0])
    sum_one, cross_query, *saved = call_front(where, tokens, vectors, layout, tiles[0])
    far_query = swap(cross_query, 2)
    own_part = call_cross_forward(infos[0], cross_query, key_table, value_table, 0)
    far_part = call_cross_forward(infos[1], far_query, key_table, value_table, slots)
    other_part = swap(far_part, 2)
    place = me[None].astype(jnp.int32)
    out_tokens, grad_two, packed, vectors_mid, keep_mid, send_mid = call_middle(
        where, place, sum_one, own_part, other_part, vectors, live.astype(F32)[:, None],
        cotangent, tiles,
    )
    far_packed = swap(packed, 2)
    pair_mid = added(keep_mid, swap(send_mid, 1))
    cuts = (0, 3 * ROWS, 9 * ROWS)

    def across(part):
        mine = pair_mid[:, cuts[part] : cuts[part + 1]]
        return added(mine[0], swap(mine[1], 2))

    own_grad, *own_sums, own_bias = call_cross_backward(
        infos[0], cross_query, packed, key_table, value_table, (pair_mid, pair_mid), 0
    )
    early_one = across(0)
    far_grad, *far_sums, far_bias = call_cross_backward(
        infos[1], far_query, far_packed, key_table, value_table, (own_grad, early_one), slots
    )
    early_two = across(1)
    early = jnp.concatenate([early_one, early_two], axis=0).reshape(-1, PANEL)
    bits = dp_bits()
    other_grad = swap(far_grad, 2)
    keep_table, send_table = call_table_gradient(
        infos, place, own_sums, far_sums, all_frames, early_two
    )
    *saved_heads, attended, lse = saved
    early = half_sum(early, bits[0])
    grad_one, grad_att, vectors_cross, keep_cross, send_cross = call_cross_back(
        where, place, sum_one, grad_two, attended, own_grad, other_grad, vectors, tiles,
        (keep_table, early),
    )
    early = half_sum(early, bits[1])
    pair_cross = added(
        jnp.concatenate([keep_table, keep_cross], axis=1),
        swap(jnp.concatenate([send_table, send_cross], axis=1), 1),
    )
    token_grads, vectors_last, keep_last, send_last = call_last(
        where, place, tokens, grad_one, grad_att, [*saved_heads, lse], vectors, layout, tiles,
        pair_cross,
    )
    late = jnp.concatenate(
        [added(pair_cross[0], swap(pair_cross[1], 2)), frame_sum(keep_last, send_last)], axis=0
    ).reshape(-1, PANEL)
    late = half_sum(late, bits[0])
    for bit in bits[2:]:
        early = half_sum(early, bit)
    for bit in bits[1:]:
        late = half_sum(late, bit)
    for bit in reversed(bits[1:]):
        early = both_halves(early, bit)
        late = both_halves(late, bit)
    grad_vectors = jnp.concatenate(
        [
            vectors_last[0:4],
            vectors_cross[0:4],
            own_bias[0:1] + far_bias[0:1],
            vectors_mid[0:10],
            jnp.zeros((5, D), F32),
        ],
        axis=0,
    )
    vector_total = total_sum(grad_vectors)[0 : vectors.shape[0]]
    held = ((7, *range(8, 16)), (5, 6, 4, 3, 0, 1, 2))
    halves_of, places_of = {}, {}
    base = 0
    for matrices in held:
        middle = len(matrices) * ROWS // 2
        for i in range(2 * middle):
            panel = matrices[i // ROWS] * ROWS + i % ROWS
            halves_of[panel] = i // middle
            places_of[panel] = base + i % middle
        base += middle
    panel_half = jnp.asarray([halves_of[p] for p in range(panel_total)], jnp.int32)
    panel_place = jnp.asarray([places_of[p] for p in range(panel_total)], jnp.int32)

    def slots_of(group):
        slot_ids = group * cap + jnp.arange(cap, dtype=jnp.int32)
        matches = slot_of[:, None] == slot_ids[None, :]
        half, place_ = (
            jnp.sum(jnp.where(matches, values[:, None], 0), axis=0, dtype=jnp.int32)
            for values in (panel_half, panel_place)
        )
        return half, place_, jnp.any(matches, axis=0)

    upper = (group_index // bits[0]) & 1
    half, own_place, used = slots_of(group_index)
    far_place = slots_of(group_index ^ bits[0])[1]
    got = over_dp(call_pick(far_place, early, late, vector_total), bits[0])
    row_total = row_count * group_count * frame_count
    updates = call_update(
        row_total,
        own_place,
        jnp.where(used, jnp.where(half == upper, 0, 1), 2),
        early,
        late,
        got,
        [w.transpose(0, 2, 1) for w in (master, first_moment, second_moment)],
    )
    matrix_grads, matrix_first, matrix_second, matrix_weights = (
        u.transpose(0, 2, 1) for u in updates
    )
    vector_grads = vector_total * (1.0 / math.sqrt(row_total))
    vector_first_new, vector_second_new, vector_weights = adam_update(
        vector_grads, vector_first, vector_second, vectors, RATE_VECTOR, 0.0
    )
    return (
        out_tokens,
        token_grads,
        matrix_grads,
        matrix_first,
        matrix_second,
        matrix_weights,
        vector_grads,
        vector_first_new,
        vector_second_new,
        vector_weights,
    )


def solution(mesh):
    in_specs = (
        P(("dp", "frame"), None),
        P("dp", "frame", None),
        P(("dp", "frame"), None),
        P("dp"),
        P("dp"),
        P(),
        P("dp", None, "frame"),
        P("dp", None, "frame"),
        P("dp", None, "frame"),
        P(),
        P(),
        P(),
    )
    out_specs = (
        P(("dp", "frame"), None),
        P(("dp", "frame"), None),
        P("dp", None, "frame"),
        P("dp", None, "frame"),
        P("dp", None, "frame"),
        P("dp", None, "frame"),
        P(),
        P(),
        P(),
        P(),
    )
    return jax.shard_map(body, mesh=mesh, in_specs=in_specs, out_specs=out_specs, check_vma=False)
```
